512 devices in a mesh: dp: 64 (over x, z, core), head: 8 (over y).
Axes of the slice: x: 4, y: 8, z: 8, core: 2. Of those that a mesh axis runs over, the one named last changes fastest.
Arguments:
- prompt_query: bfloat16 [4096, 8192], P('dp', 'head'), may hold values from -6 to 6
- prompt_key: bfloat16 [4096, 1024], P('dp', 'head'), may hold values from -6 to 6
- prompt_value: bfloat16 [4096, 1024], P('dp', 'head'), may hold values from -6 to 6
- prompt_out: bfloat16 [4096, 8192], P('dp', 'head'), may hold values from -6 to 6
- prompt_grad: bfloat16 [4096, 8192], P('dp', 'head'), may hold values from -40 to 40
- response_query: bfloat16 [64, 64, 8192], P('dp', None, 'head'), may hold values from -6 to 6
- response_key: bfloat16 [64, 64, 1024], P('dp', None, 'head'), may hold values from -6 to 6
- response_value: bfloat16 [64, 64, 1024], P('dp', None, 'head'), may hold values from -6 to 6
- response_out: bfloat16 [64, 64, 8192], P('dp', None, 'head'), may hold values from -6 to 6
- response_grad: bfloat16 [64, 64, 8192], P('dp', None, 'head'), may hold values from -40 to 40
- lengths: int32 [64], P('dp'), may hold values from 1 to 64, 2560 in all
- query_gain: float32 [128], replicated, may hold values from 0.6 to 6
- key_gain: float32 [128], replicated, may hold values from 0.6 to 6
Outputs:
- prompt_dquery: bfloat16 [4096, 8192], P('dp', 'head')
- prompt_dkey: bfloat16 [4096, 1024], P('dp', 'head')
- prompt_dvalue: bfloat16 [4096, 1024], P('dp', 'head')
- response_dquery: bfloat16 [64, 64, 8192], P('dp', None, 'head')
- response_dkey: bfloat16 [64, 64, 1024], P('dp', None, 'head')
- response_dvalue: bfloat16 [64, 64, 1024], P('dp', None, 'head')
- query_dgain: float32 [128], replicated
- key_dgain: float32 [128], replicated
The draws below stay inside these ranges and needn't reach their ends.
Inputs may be any that keep to these rules, and one draw needn't show every extreme that they name: `lengths`: some response has all 64 tokens live.
All inputs are finite; a program needn't handle non-finite values. No bound on the sum of `lengths` on one device may be relied on, other than what follows from the above.
Results may differ from the reference program's by a relative error of at most 0.012.
The reference program's roundings to bfloat16 on the way count: a program that leaves them out, or rounds other values in their place, can miss the bound.
Values may be sent and summed in bfloat16 or wider, within the bound.
No kernel may reach another device: no remote copies, remote signals or barrier semaphores. Data moves between devices by JAX's collectives and lax.ppermute only.
A program may use at most 64 MiB of HBM per device.

```python
import math
from functools import reduce
import jax
import jax.numpy as jnp
import numpy as np
from jax import lax

HD = 128
GROUPQ = 8
RLEN = 64
KV_HEADS = 8
QHEADS = 64
PTOK = 4096
RESP = 64


def prompt_key_draw(key):
    key = jax.random.fold_in(key, 40)
    first, second = jax.random.split(key)
    base = jnp.clip(jax.random.normal(first, (PTOK, KV_HEADS * HD), jnp.float32), -5.0, 5.0)
    noise = jax.random.normal(second, (PTOK, KV_HEADS * HD), jnp.float32)
    rows = jnp.arange(PTOK)[:, None] % 16
    near = jnp.where(rows == 3, jnp.roll(base, -1, axis=0) + 0.15 * noise, base)
    return jnp.clip(near, -6.0, 6.0)


def response_key_draw(key):
    key = jax.random.fold_in(key, 50)
    first, second = jax.random.split(key)
    base = jnp.clip(jax.random.normal(first, (RESP, RLEN, KV_HEADS * HD), jnp.float32), -5.0, 5.0)
    noise = jax.random.normal(second, (RESP, RLEN, KV_HEADS * HD), jnp.float32)
    rows = jnp.arange(RLEN)[None, :, None] % 16
    near = jnp.where(rows == 3, jnp.roll(base, -1, axis=1) + 0.15 * noise, base)
    return jnp.clip(near, -6.0, 6.0)


def draw_prompt_key(key, part):
    return prompt_key_draw(key).astype(jnp.bfloat16)


def draw_response_key(key, part):
    return response_key_draw(key).astype(jnp.bfloat16)


def draw_prompt_query(key, part):
    key = jax.random.fold_in(key, 1)
    values = jnp.clip(jax.random.normal(key, (PTOK, QHEADS * HD), jnp.float32), -6.0, 6.0)
    return values.astype(jnp.bfloat16)


def draw_response_query(key, part):
    key = jax.random.fold_in(key, 2)
    values = jnp.clip(jax.random.normal(key, (RESP, RLEN, QHEADS * HD), jnp.float32), -6.0, 6.0)
    return values.astype(jnp.bfloat16)


def draw_prompt_grad(key, part):
    key = jax.random.fold_in(key, 21)
    first, second = jax.random.split(key, 2)
    ramp = 1.0 + 2.0 * jnp.arange(PTOK, dtype=jnp.float32) / PTOK
    spread = jnp.exp(jax.random.uniform(second, (PTOK, 1), jnp.float32, -1.15, 1.15))
    base = jnp.clip(jax.random.normal(first, (PTOK, QHEADS * HD), jnp.float32), -4.0, 4.0)
    return (base * ramp[:, None] * spread).astype(jnp.bfloat16)


def draw_response_grad(key, part):
    key = jax.random.fold_in(key, 22)
    first, second = jax.random.split(key, 2)
    ramp = 1.0 + 2.0 * jnp.arange(RESP, dtype=jnp.float32) / RESP
    spread = jnp.exp(jax.random.uniform(second, (RESP, RLEN, 1), jnp.float32, -1.15, 1.15))
    base = jnp.clip(jax.random.normal(first, (RESP, RLEN, QHEADS * HD), jnp.float32), -4.0, 4.0)
    return (base * ramp[:, None, None] * spread).astype(jnp.bfloat16)


def draw_query_gain(key, part):
    key = jax.random.fold_in(key, 31)
    return jnp.exp(jax.random.uniform(key, (HD,), jnp.float32, math.log(0.6), math.log(1.6)))


def draw_key_gain(key, part):
    key = jax.random.fold_in(key, 32)
    return jnp.exp(jax.random.uniform(key, (HD,), jnp.float32, math.log(0.6), math.log(1.6)))


def levels(own_key, extent, cuts, low, largest):
    def one(axis_at, parts):
        steps = jax.random.uniform(jax.random.fold_in(jax.random.fold_in(own_key, 6), axis_at), (parts,), jnp.float32, low / len(cuts), largest / len(cuts))
        return jnp.repeat(jnp.exp(steps), extent[axis_at] // parts).reshape((-1,) + (1,) * (len(extent) - axis_at - 1))

    level = one(*cuts[0])
    for cut in cuts[1:]:
        level = level * one(*cut)
    return level


def split_up(number_of, total, bound, slope):
    loads = [(1 << 20) // math.isqrt(rank ** slope) + 1 for rank in range(2, number_of + 1)]
    surplus, counts = total - bound - (number_of - 1), [1] * (number_of - 1)
    while surplus > 0:
        candidates = [i for i in range(number_of - 1) if counts[i] < bound]
        mass, remaining = sum([loads[i] for i in candidates]), surplus
        for i in candidates:
            addition = min(bound - counts[i], max(1, remaining * loads[i] // mass), surplus)
            counts[i] = counts[i] + addition
            surplus = surplus - addition
    return np.array([bound] + counts)


def ragged_sizes(rng, count, total, reach, skew):
    if count == 2:
        one = jax.random.randint(rng, (), max(1, total - reach), min(reach, total - 1) + 1)
        return jnp.stack([one, total - one])
    tallies = jnp.asarray(split_up(count, total, reach, skew), jnp.int32)
    twos = (count - 1) // 2
    donor, sink = tallies[1:1 + 2 * twos:2], tallies[2:2 + 2 * twos:2]
    room = jnp.minimum(donor - 1, reach - sink)
    passed = jax.random.randint(jax.random.fold_in(rng, 1), (twos,), 0, 1 << 20) % (room + 1)
    tallies = tallies.at[1:1 + 2 * twos:2].set(donor - passed).at[2:2 + 2 * twos:2].set(sink + passed)
    return tallies[jax.random.permutation(jax.random.fold_in(rng, 2), count)]


def gaussian(own_key, dims, deviation, limit, cuts=(), held_as=jnp.bfloat16):
    level = levels(own_key, dims, cuts, -0.22, 0.18) if cuts else 1.0
    drawn = jax.random.normal(own_key, dims, jnp.float32) * deviation * level
    return jnp.minimum(jnp.maximum(drawn, -limit), limit).astype(held_as)


def setup_inputs(seed: int = 0) -> dict:
    streams_of = jax.random.split(jax.random.key(seed), 14)
    return {
        "prompt_query": draw_prompt_query(jax.random.fold_in(streams_of[13], 71), 0),
        "prompt_key": draw_prompt_key(jax.random.fold_in(streams_of[13], 71), 0),
        "prompt_value": gaussian(streams_of[2], (PTOK, KV_HEADS * HD), 1.0, 6.0, ((0, 64), (1, 8))),
        "prompt_out": gaussian(streams_of[3], (PTOK, QHEADS * HD), 1.0, 6.0, ((0, 64), (1, 8))),
        "prompt_grad": draw_prompt_grad(jax.random.fold_in(streams_of[13], 71), 0),
        "response_query": draw_response_query(jax.random.fold_in(streams_of[13], 71), 0),
        "response_key": draw_response_key(jax.random.fold_in(streams_of[13], 71), 0),
        "response_value": gaussian(streams_of[7], (RESP, RLEN, KV_HEADS * HD), 1.0, 6.0, ((0, 64), (2, 8))),
        "response_out": gaussian(streams_of[8], (RESP, RLEN, QHEADS * HD), 1.0, 6.0, ((0, 64), (2, 8))),
        "response_grad": draw_response_grad(jax.random.fold_in(streams_of[13], 71), 0),
        "lengths": ragged_sizes(streams_of[10], RESP, RESP * RLEN * 5 // 8, RLEN, 2).astype(jnp.int32),
        "query_gain": draw_query_gain(jax.random.fold_in(streams_of[13], 71), 0),
        "key_gain": draw_key_gain(jax.random.fold_in(streams_of[13], 71), 0),
    }


epsilon = 1e-06
masked_value = -1e+30

def rounded(values):
    return lax.optimization_barrier(values.astype(jnp.bfloat16))

def product(form, left, right):
    return jnp.einsum(form, left.astype(jnp.float32), right.astype(jnp.float32))

def normalize(raw, gain):
    values = raw.astype(jnp.float32)
    inverse = lax.rsqrt(lax.optimization_barrier(jnp.mean(values * values, axis=-1, keepdims=True)) + epsilon)
    unit_rows = values * inverse
    return (rounded(unit_rows * gain), unit_rows, inverse)

def norm_back(unit_rows, inverse, grads, gain):
    scaled = grads * gain
    return inverse * (scaled - unit_rows * lax.optimization_barrier(jnp.mean(unit_rows * scaled, axis=-1, keepdims=True)))

def attend_back(queries, grad_out, saved_out, key_parts, value_parts, mask_parts, living):
    scaling = 1.0 / math.sqrt(queries.shape[-1])
    scores = [jnp.where(mask_part[None], product('qgd,kd->gqk', queries, key_part) * scaling, masked_value) for key_part, mask_part in zip(key_parts, mask_parts)]
    row_max = reduce(jnp.maximum, [lax.optimization_barrier(jnp.max(part, axis=-1)) for part in scores])
    raised = [jnp.where(mask_part[None], jnp.exp(part - row_max[..., None]), 0.0) for part, mask_part in zip(scores, mask_parts)]
    totals = sum((lax.optimization_barrier(jnp.sum(part, axis=-1)) for part in raised)) + (1.0 - living)[None]
    deltas = lax.optimization_barrier(jnp.sum(grad_out.astype(jnp.float32) * saved_out.astype(jnp.float32), axis=-1)).T
    dquery = jnp.zeros(queries.shape, jnp.float32)
    dkeys = []
    dvalues = []
    for part, key_part, value_part in zip(raised, key_parts, value_parts):
        weights = part / totals[..., None]
        dweights = product('qgd,kd->gqk', grad_out, value_part)
        dscores = weights * (dweights - deltas[..., None])
        weights_b = rounded(weights)
        dscores_b = rounded(dscores)
        dvalues.append(product('gqk,qgd->kd', weights_b, grad_out))
        dkeys.append(product('gqk,qgd->kd', dscores_b, queries) * scaling)
        dquery = dquery + product('gqk,kd->qgd', dscores_b, key_part) * scaling
    return (dquery, dkeys, dvalues)

def reference(prompt_query, prompt_key, prompt_value, prompt_out, prompt_grad, response_query, response_key, response_value, response_out, response_grad, lengths, query_gain, key_gain):
    shaped_pquery = prompt_query.reshape(PTOK, KV_HEADS, GROUPQ, HD)
    shaped_pgrad = prompt_grad.reshape(PTOK, KV_HEADS, GROUPQ, HD)
    shaped_pout = prompt_out.reshape(PTOK, KV_HEADS, GROUPQ, HD)
    shaped_rquery = response_query.reshape(RESP, RLEN, KV_HEADS, GROUPQ, HD)
    shaped_rgrad = response_grad.reshape(RESP, RLEN, KV_HEADS, GROUPQ, HD)
    shaped_rout = response_out.reshape(RESP, RLEN, KV_HEADS, GROUPQ, HD)
    positions = jnp.arange(RLEN)
    causal = positions[:, None] >= positions[None, :]
    prompt_pos = jnp.arange(PTOK)
    prompt_mask = prompt_pos[None, :] <= prompt_pos[:, None]
    query_sum = jnp.zeros((HD,), jnp.float32)
    key_sum = jnp.zeros((HD,), jnp.float32)
    outs_pq, outs_pk, outs_pv, outs_rq, outs_rk, outs_rv = ([], [], [], [], [], [])
    for head_group in range(KV_HEADS):
        columns = slice(head_group * HD, (head_group + 1) * HD)
        pq_normed, pq_unit, pq_inverse = normalize(shaped_pquery[:, head_group], query_gain)
        pk_normed, pk_unit, pk_inverse = normalize(prompt_key[:, columns], key_gain)
        prompt_vals = prompt_value[:, columns]
        rq_normed, rq_unit, rq_inverse = normalize(shaped_rquery[:, :, head_group], query_gain)
        rk_normed, rk_unit, rk_inverse = normalize(response_key[:, :, columns], key_gain)
        resp_vals = response_value[:, :, columns]
        prompt_dq, dkeys, dvalues = attend_back(pq_normed, shaped_pgrad[:, head_group], shaped_pout[:, head_group], [pk_normed], [prompt_vals], [prompt_mask], jnp.ones((PTOK,), jnp.float32))
        collected = jnp.concatenate([dkeys[0], dvalues[0]], axis=1)

        def one_response(collected, item):
            q_one, grad_one, out_one, key_one, value_one, length_one = item
            living = positions < length_one
            mask_parts = [jnp.broadcast_to(living[:, None], (RLEN, PTOK)), living[:, None] & causal]
            dquery, dkeys, dvalues = attend_back(q_one, grad_one, out_one, [pk_normed, key_one], [prompt_vals, value_one], mask_parts, living.astype(jnp.float32))
            collected = collected + jnp.concatenate([dkeys[0], dvalues[0]], axis=1)
            return (collected, (dquery, dkeys[1], dvalues[1]))
        collected, (resp_dq, resp_dk, resp_dv) = lax.scan(one_response, collected, (rq_normed, shaped_rgrad[:, :, head_group], shaped_rout[:, :, head_group], rk_normed, resp_vals, lengths))
        prompt_dk = collected[:, :HD]
        outs_pq.append(norm_back(pq_unit, pq_inverse, prompt_dq, query_gain).astype(jnp.bfloat16))
        outs_pk.append(norm_back(pk_unit, pk_inverse, prompt_dk, key_gain).astype(jnp.bfloat16))
        outs_pv.append(collected[:, HD:].astype(jnp.bfloat16))
        outs_rq.append(norm_back(rq_unit, rq_inverse, resp_dq, query_gain).astype(jnp.bfloat16))
        outs_rk.append(norm_back(rk_unit, rk_inverse, resp_dk, key_gain).astype(jnp.bfloat16))
        outs_rv.append(resp_dv.astype(jnp.bfloat16))
        query_sum = query_sum + lax.optimization_barrier(jnp.sum(prompt_dq * pq_unit, axis=(0, 1))) + lax.optimization_barrier(jnp.sum(resp_dq * rq_unit, axis=(0, 1, 2)))
        key_sum = key_sum + lax.optimization_barrier(jnp.sum(prompt_dk * pk_unit, axis=0)) + lax.optimization_barrier(jnp.sum(resp_dk * rk_unit, axis=(0, 1)))
    prompt_dquery = jnp.stack(outs_pq, axis=1).reshape(PTOK, QHEADS * HD)
    prompt_dkey = jnp.concatenate(outs_pk, axis=1)
    prompt_dvalue = jnp.concatenate(outs_pv, axis=1)
    response_dquery = jnp.stack(outs_rq, axis=2).reshape(RESP, RLEN, QHEADS * HD)
    response_dkey = jnp.concatenate(outs_rk, axis=2)
    response_dvalue = jnp.concatenate(outs_rv, axis=2)
    return (prompt_dquery, prompt_dkey, prompt_dvalue, response_dquery, response_dkey, response_dvalue, query_sum, key_sum)
```

```python
import functools
import math

import jax
import jax.numpy as jnp
from jax import lax
from jax.experimental import pallas as pl
from jax.experimental.pallas import tpu as pltpu
from jax.sharding import Mesh
from jax.sharding import PartitionSpec as P

NX, NZ, NC = 4, 8, 2
HD = 128
GROUPS = 8
ROWS = 64
PCOLS = GROUPS * ROWS
COLS = 2 * PCOLS
BLOCKS = NX * NZ * NC
KEYS = BLOCKS * ROWS
HALF = KEYS // 2
CHUNK = NZ * ROWS
CG = 256
EXTRA = 8
TAIL = 16
INTERPRET = False
epsilon = 1e-06
masked_value = -1e30
SCALING = 1.0 / math.sqrt(HD)
EXP_SCALE = SCALING * math.log2(math.e)


def unit_rows(values):
    inverse = lax.rsqrt(jnp.mean(values * values, axis=-1, keepdims=True) + epsilon)
    return values * inverse, inverse


def norm_back(unit, inverse, grads, gain):
    scaled = grads * gain
    return inverse * (scaled - unit * jnp.mean(unit * scaled, axis=-1, keepdims=True))


def mm(left, right):
    return jnp.dot(left, right, preferred_element_type=jnp.float32)


def two_heads(ref, pair):
    first = ref[:, 2 * pair * HD : (2 * pair + 1) * HD]
    second = ref[:, (2 * pair + 1) * HD : (2 * pair + 2) * HD]
    return jnp.concatenate([first.astype(jnp.float32), second.astype(jnp.float32)], axis=0)


def prepare_kernel(pq_in, pg_in, po_in, rq_in, rg_in, ro_in, qgain, qn, qn_t, gr, gr_t, delta, held, sems):
    f32, bf16 = jnp.float32, jnp.bfloat16
    copies = [
        pltpu.make_async_copy(ref, held.at[i], sems.at[i])
        for i, ref in enumerate((pq_in, rq_in, pg_in, rg_in, po_in, ro_in))
    ]
    for copy in copies:
        copy.start()
    for copy in copies:
        copy.wait()
    gain_q = qgain[...]
    for part in range(2):
        q, g, o = held.at[part], held.at[2 + part], held.at[4 + part]
        for pair in range(GROUPS // 2):
            r0 = part * PCOLS + pair * 2 * ROWS
            rows = slice(r0, r0 + 2 * ROWS)
            unit, _ = unit_rows(two_heads(q, pair))
            normed = (unit * gain_q).astype(bf16)
            qn[rows, :] = normed
            qn_t[:, rows] = normed.astype(f32).T.astype(bf16)
            grads = two_heads(g, pair)
            gr[rows, :] = grads.astype(bf16)
            gr_t[:, rows] = grads.T.astype(bf16)
            product = grads * two_heads(o, pair)
            delta[:, rows] = jnp.sum(product.T, axis=0, keepdims=True)


def prepare(arrays, qgain):
    f32, bf16 = jnp.float32, jnp.bfloat16
    vmem = pl.BlockSpec(memory_space=pltpu.VMEM)
    out_shape = (
        jax.ShapeDtypeStruct((COLS, HD), bf16),
        jax.ShapeDtypeStruct((HD, COLS), bf16),
        jax.ShapeDtypeStruct((COLS, HD), bf16),
        jax.ShapeDtypeStruct((HD, COLS), bf16),
        jax.ShapeDtypeStruct((1, COLS), f32),
    )
    return pl.pallas_call(
        prepare_kernel,
        out_shape=out_shape,
        in_specs=[pl.BlockSpec(memory_space=pl.ANY)] * len(arrays) + [vmem],
        out_specs=tuple([vmem] * len(out_shape)),
        scratch_shapes=[
            pltpu.VMEM((len(arrays), ROWS, GROUPS * HD), bf16),
            pltpu.SemaphoreType.DMA((len(arrays),)),
        ],
        compiler_params=pltpu.CompilerParams(vmem_limit_bytes=8 * 1024 * 1024),
        cost_estimate=pl.CostEstimate(flops=COLS * HD * 40, bytes_accessed=2 << 20, transcendentals=0),
        interpret=INTERPRET,
    )(*arrays, qgain)


def attention_kernel(
    info, pq_in, rq_in, rk_in, rv_in, qn, qn_t, gr, gr_t, delta, kv_own, kv_other, qgain, kgain,
    keep, send, terms, pdq, rdq, rdk, rdv,
    kn, kn_t, vals, kunit, rkn, rkn_t, probs, rprobs, maxima, top, total, factor, dq_t, held, rk, rv,
    sems,
):
    f32, bf16 = jnp.float32, jnp.bfloat16
    kv_refs = (kv_own, kv_other)
    gain_q, gain_k = qgain[...], kgain[...]
    copies = [
        pltpu.make_async_copy(rk_in, rk, sems.at[0]),
        pltpu.make_async_copy(rv_in, rv, sems.at[1]),
        pltpu.make_async_copy(pq_in, held.at[0], sems.at[2]),
        pltpu.make_async_copy(rq_in, held.at[1], sems.at[3]),
    ]
    for copy in copies:
        copy.start()

    k0 = 0
    for ref in kv_refs:
        for at in range(0, ref.shape[0], CHUNK):
            rows = slice(k0, k0 + CHUNK)
            unit, _ = unit_rows(ref[at : at + CHUNK, :HD].astype(f32))
            normed = (unit * gain_k).astype(bf16)
            kunit[rows, :] = unit
            kn[rows, :] = normed
            kn_t[k0 // CHUNK] = normed.astype(f32).T.astype(bf16)
            vals[rows, :] = ref[at : at + CHUNK, HD:]
            k0 += CHUNK

    copies[0].wait()
    copies[1].wait()
    runit, rinv = unit_rows(rk[...].astype(f32))
    rnormed = (runit * gain_k).astype(bf16)
    rkn[...] = rnormed
    rkn_t[...] = rnormed.astype(f32).T.astype(bf16)

    scores = mm(rkn[...], qn_t[:, PCOLS:]) * EXP_SCALE
    key_at = lax.broadcasted_iota(jnp.int32, (ROWS, PCOLS), 0)
    query_at = lax.broadcasted_iota(jnp.int32, (ROWS, PCOLS), 1) & (ROWS - 1)
    scores = jnp.where(key_at <= query_at, scores, masked_value)
    first = jnp.max(scores, axis=0, keepdims=True)
    raised = jnp.exp2(scores - first)
    rprobs[...] = raised
    rfirst = first
    top[:, :PCOLS] = jnp.full((1, PCOLS), masked_value, f32)
    total[:, :PCOLS] = jnp.zeros((1, PCOLS), f32)
    top[:, PCOLS:] = first
    total[:, PCOLS:] = jnp.sum(raised, axis=0, keepdims=True)

    my_x, my_z, my_core = info[1], info[2], info[3]

    def first_pass(j, _):
        at = pl.multiple_of(j * CHUNK, CHUNK)
        key_x = lax.rem(j, NX)
        key_core = jnp.where(j < NX, my_core, 1 - my_core)

        def tile(c0, masked):
            cols = slice(c0, c0 + CG)
            scores = mm(kn[pl.ds(at, CHUNK), :], qn_t[:, cols]) * EXP_SCALE
            if masked:
                row = lax.broadcasted_iota(jnp.int32, (CHUNK, 1), 0)
                key_block = (key_x * NZ + row // ROWS) * NC + key_core
                key_pos = key_block * ROWS + (row & (ROWS - 1))
                query_pos = lax.broadcasted_iota(jnp.int32, (1, CG), 1) & (ROWS - 1)
                query_pos = query_pos + ((my_x * NZ + my_z) * NC + my_core) * ROWS
                scores = jnp.where(key_pos <= query_pos, scores, masked_value)
            old = top[:, cols]
            new = jnp.maximum(old, jnp.max(scores, axis=0, keepdims=True))
            raised = jnp.exp2(scores - new)
            probs[pl.ds(at, CHUNK), cols] = raised
            total[:, cols] = total[:, cols] * jnp.exp2(old - new) + jnp.sum(
                raised, axis=0, keepdims=True
            )
            top[:, cols] = new
            maxima[j, :, cols] = new

        @pl.when(key_x < my_x)
        def _():
            for c0 in range(0, COLS, CG):
                tile(c0, False)

        @pl.when(key_x >= my_x)
        def _():
            for c0 in range(0, COLS, CG):
                tile(c0, c0 < PCOLS)

        return 0

    lax.fori_loop(0, KEYS // CHUNK, first_pass, 0)

    column = lax.broadcasted_iota(jnp.int32, (1, COLS), 1)
    living = (column < PCOLS) | ((column & (ROWS - 1)) < info[0])
    factor[...] = jnp.where(living, 1.0 / total[...], 0.0)
    dq_t[...] = jnp.zeros_like(dq_t)

    def second_pass(out, base, j, carry):
        key_terms, largest_k, largest_v = carry
        at = pl.multiple_of(j * CHUNK, CHUNK)
        here = pl.multiple_of((j - base) * CHUNK, CHUNK)
        values = vals[pl.ds(at, CHUNK), :]
        keys_t = kn_t[j]
        dkey = jnp.zeros((CHUNK, HD), f32)
        dvalue = jnp.zeros((CHUNK, HD), f32)
        for c0 in range(0, COLS, CG):
            cols = slice(c0, c0 + CG)
            scale = jnp.exp2(maxima[j, :, cols] - top[:, cols]) * factor[:, cols]
            weights = probs[pl.ds(at, CHUNK), cols] * scale
            dweights = mm(values, gr_t[:, cols])
            dscores = (weights * (dweights - delta[:, cols])).astype(bf16)
            dvalue = dvalue + mm(weights.astype(bf16), gr[cols, :])
            dkey = dkey + mm(dscores, qn[cols, :])
            dq_t[:, cols] = dq_t[:, cols] + mm(keys_t, dscores)
        dkey = dkey * SCALING
        out[pl.ds(here, CHUNK), :HD] = dkey
        out[pl.ds(here, CHUNK), HD:] = dvalue
        products = dkey * kunit[pl.ds(at, CHUNK), :]
        eights = (CHUNK // 8, 8, HD)
        return (
            key_terms + jnp.sum(products.reshape(eights), axis=0),
            jnp.maximum(largest_k, jnp.max(jnp.abs(dkey).reshape(eights), axis=0)),
            jnp.maximum(largest_v, jnp.max(jnp.abs(dvalue).reshape(eights), axis=0)),
        )

    half = HALF // CHUNK
    zero = jnp.zeros((8, HD), f32)
    key_terms = zero
    for out, base in ((send, half), (keep, 0)):
        key_terms, largest_k, largest_v = lax.fori_loop(
            base, base + half, functools.partial(second_pass, out, base), (key_terms, zero, zero)
        )
        out[HALF:, :HD] = jnp.broadcast_to(jnp.max(largest_k, axis=0, keepdims=True), (EXTRA, HD))
        out[HALF:, HD:] = jnp.broadcast_to(jnp.max(largest_v, axis=0, keepdims=True), (EXTRA, HD))

    right = slice(PCOLS, COLS)
    scale = jnp.exp2(rfirst - top[:, right]) * factor[:, right]
    weights = rprobs[...] * scale
    dweights = mm(rv[...], gr_t[:, right])
    dscores = (weights * (dweights - delta[:, right])).astype(bf16)
    rdv[...] = mm(weights.astype(bf16), gr[right, :]).astype(bf16)
    dkey = mm(dscores, qn[right, :]) * SCALING
    rdk[...] = norm_back(runit, rinv, dkey, gain_k).astype(bf16)
    dq_t[:, right] = dq_t[:, right] + mm(rkn_t[...], dscores)
    key_terms = jnp.sum(key_terms, axis=0, keepdims=True)
    key_terms = key_terms + jnp.sum(dkey * runit, axis=0, keepdims=True)

    query_terms = jnp.zeros((1, HD), f32)
    copies[2].wait()
    copies[3].wait()
    for part, out in enumerate((pdq, rdq)):
        q = held.at[part]
        for pair in range(GROUPS // 2):
            r0 = part * PCOLS + pair * 2 * ROWS
            unit, inverse = unit_rows(two_heads(q, pair))
            dquery = dq_t[:, r0 : r0 + 2 * ROWS].T * SCALING
            query_terms = query_terms + jnp.sum(dquery * unit, axis=0, keepdims=True)
            raw = norm_back(unit, inverse, dquery, gain_q).astype(bf16)
            out[:, 2 * pair * HD : (2 * pair + 1) * HD] = raw[:ROWS]
            out[:, (2 * pair + 1) * HD : (2 * pair + 2) * HD] = raw[ROWS:]

    terms[:, :HD] = jnp.broadcast_to(query_terms, (EXTRA, HD))
    terms[:, HD:] = jnp.broadcast_to(key_terms, (EXTRA, HD))


def attention(info, raw, arrays):
    f32, bf16 = jnp.float32, jnp.bfloat16
    vmem = pl.BlockSpec(memory_space=pltpu.VMEM)
    smem = pl.BlockSpec(memory_space=pltpu.SMEM)
    anywhere = pl.BlockSpec(memory_space=pl.ANY)
    out_shape = (
        jax.ShapeDtypeStruct((HALF + EXTRA, 2 * HD), f32),
        jax.ShapeDtypeStruct((HALF + EXTRA, 2 * HD), f32),
        jax.ShapeDtypeStruct((EXTRA, 2 * HD), f32),
        jax.ShapeDtypeStruct((ROWS, GROUPS * HD), bf16),
        jax.ShapeDtypeStruct((ROWS, GROUPS * HD), bf16),
        jax.ShapeDtypeStruct((ROWS, HD), bf16),
        jax.ShapeDtypeStruct((ROWS, HD), bf16),
    )
    chunks = KEYS // CHUNK
    scratch = [
        pltpu.VMEM((KEYS, HD), bf16),
        pltpu.VMEM((chunks, HD, CHUNK), bf16),
        pltpu.VMEM((KEYS, HD), bf16),
        pltpu.VMEM((KEYS, HD), f32),
        pltpu.VMEM((ROWS, HD), bf16),
        pltpu.VMEM((HD, ROWS), bf16),
        pltpu.VMEM((KEYS, COLS), f32),
        pltpu.VMEM((ROWS, PCOLS), f32),
        pltpu.VMEM((chunks, 1, COLS), f32),
        pltpu.VMEM((1, COLS), f32),
        pltpu.VMEM((1, COLS), f32),
        pltpu.VMEM((1, COLS), f32),
        pltpu.VMEM((HD, COLS), f32),
        pltpu.VMEM((2, ROWS, GROUPS * HD), bf16),
        pltpu.VMEM((ROWS, HD), bf16),
        pltpu.VMEM((ROWS, HD), bf16),
        pltpu.SemaphoreType.DMA((4,)),
    ]
    return pl.pallas_call(
        attention_kernel,
        out_shape=out_shape,
        in_specs=[smem] + [anywhere] * len(raw) + [vmem] * len(arrays),
        out_specs=tuple([vmem] * len(out_shape)),
        scratch_shapes=scratch,
        compiler_params=pltpu.CompilerParams(vmem_limit_bytes=48 * 1024 * 1024),
        cost_estimate=pl.CostEstimate(
            flops=10 * KEYS * COLS * HD, bytes_accessed=8 << 20, transcendentals=KEYS * COLS
        ),
        interpret=INTERPRET,
    )(info, *raw, *arrays)


def exchange(array, axis):
    return lax.all_to_all(array, axis, 0, 0, tiled=True)


def exchange_halves(message, axis):
    halves = message.astype(jnp.float16).reshape(-1, 2 * HD)
    return exchange(halves, axis).astype(jnp.float32).reshape(message.shape)


def swap_core(array):
    return lax.ppermute(array, "core", [(0, 1), (1, 0)])


def pack_message(message, rows, count, blocks, largest, terms):
    exponent = jnp.clip(jnp.floor(jnp.log2(jnp.maximum(largest, 1e-37))), -100.0, 100.0)
    scale = jnp.exp2(14.0 - exponent)
    term_exponent = jnp.clip(
        jnp.floor(jnp.log2(jnp.maximum(jnp.abs(terms), 1e-37))), -100.0, 100.0
    )
    scaled = terms * jnp.exp2(14.0 - term_exponent)
    high = scaled.astype(jnp.bfloat16).astype(jnp.float32)
    low = (scaled - high) * 256.0
    row = lax.broadcasted_iota(jnp.int32, (TAIL, 2 * HD), 0)
    tail = jnp.where(row == 2, exponent, term_exponent)
    tail = jnp.where(row == 0, high, jnp.where(row == 1, low, tail))
    for i in range(count):
        message[i, :rows] = blocks(i) * scale
        message[i, rows:] = tail


def unpack_message(message, rows, count):
    total = jnp.zeros((rows, 2 * HD), jnp.float32)
    terms = jnp.zeros((1, 2 * HD), jnp.float32)
    for i in range(count):
        tail = message[i, rows:]
        total = total + message[i, :rows] * jnp.exp2(tail[2:3] - 14.0)
        terms = terms + (tail[0:1] + tail[1:2] * (1.0 / 256.0)) * jnp.exp2(tail[3:4] - 14.0)
    return total, terms


def first_stage_kernel(keep, got, terms, message):
    rows = NZ * ROWS
    largest = keep[HALF : HALF + 1, :] + got[HALF : HALF + 1, :]

    def blocks(i):
        return keep[i * rows : (i + 1) * rows, :] + got[i * rows : (i + 1) * rows, :]

    pack_message(message, rows, NX, blocks, largest, terms[0:1, :])


def second_stage_kernel(got, message):
    total, terms = unpack_message(got, NZ * ROWS, NX)
    largest = jnp.max(jnp.abs(total), axis=0, keepdims=True)
    pack_message(message, ROWS, NZ, lambda i: total[i * ROWS : (i + 1) * ROWS], largest, terms)


def last_stage_kernel(got, keys, kgain, pdk, pdv, query_terms, key_terms):
    total, terms = unpack_message(got, ROWS, NZ)
    unit, inverse = unit_rows(keys[...].astype(jnp.float32))
    pdk[...] = norm_back(unit, inverse, total[:, :HD], kgain[...]).astype(jnp.bfloat16)
    pdv[...] = total[:, HD:].astype(jnp.bfloat16)
    query_terms[...] = terms[:, :HD]
    key_terms[...] = terms[:, HD:]


def small_kernel(body, out_shape, *arrays):
    vmem = pl.BlockSpec(memory_space=pltpu.VMEM)
    outs = vmem if isinstance(out_shape, jax.ShapeDtypeStruct) else tuple([vmem] * len(out_shape))
    return pl.pallas_call(
        body,
        out_shape=out_shape,
        in_specs=[vmem] * len(arrays),
        out_specs=outs,
        compiler_params=pltpu.CompilerParams(vmem_limit_bytes=16 * 1024 * 1024),
        cost_estimate=pl.CostEstimate(flops=1 << 20, bytes_accessed=4 << 20, transcendentals=0),
        interpret=INTERPRET,
    )(*arrays)


def sum_over_heads(terms):
    heads = lax.axis_size("head")
    step = 1
    while step < heads:
        pairs = [(i, i ^ step) for i in range(heads)]
        terms = terms + lax.ppermute(terms, "head", pairs)
        step *= 2
    return terms + swap_core(terms)


def per_device(
    prompt_query,
    prompt_key,
    prompt_value,
    prompt_out,
    prompt_grad,
    response_query,
    response_key,
    response_value,
    response_out,
    response_grad,
    lengths,
    query_gain,
    key_gain,
):
    line = NX * NZ
    place = [lax.axis_index(name).astype(jnp.int32)[None] for name in ("x", "z", "core")]
    info = jnp.concatenate([lengths, *place])
    qgain, kgain = query_gain.reshape(1, HD), key_gain.reshape(1, HD)

    local = jnp.concatenate([prompt_key, prompt_value], axis=1)
    copies = jnp.broadcast_to(local[None], (line,) + local.shape)
    own = exchange(copies.reshape(line * ROWS, 2 * HD), ("x", "z"))
    raw = [prompt_query, prompt_grad, prompt_out, response_query[0], response_grad[0], response_out[0]]
    prepared = prepare(raw, qgain)
    own, prepared = lax.optimization_barrier((own, prepared))
    other = swap_core(own)
    keep, give, terms, pdq, rdq, rdk, rdv = attention(
        info,
        [prompt_query, response_query[0], response_key[0], response_value[0]],
        [*prepared, own, other, qgain, kgain],
    )

    got = swap_core(give)
    terms = sum_over_heads(terms)
    rows = NZ * ROWS + TAIL
    message = small_kernel(
        first_stage_kernel, jax.ShapeDtypeStruct((NX, rows, 2 * HD), jnp.float32), keep, got, terms
    )
    message = exchange_halves(message, "x")
    rows = ROWS + TAIL
    message = small_kernel(
        second_stage_kernel, jax.ShapeDtypeStruct((NZ, rows, 2 * HD), jnp.float32), message
    )
    message = exchange_halves(message, "z")
    block = jax.ShapeDtypeStruct((ROWS, HD), jnp.bfloat16)
    gain = jax.ShapeDtypeStruct((1, HD), jnp.float32)
    pdk, pdv, query_total, key_total = small_kernel(
        last_stage_kernel, (block, block, gain, gain), message, prompt_key, kgain
    )
    return pdq, pdk, pdv, rdq[None], rdk[None], rdv[None], query_total[0], key_total[0]


def solution(mesh):
    heads = mesh.devices.shape[1]
    mesh = Mesh(mesh.devices.reshape(NX, NZ, NC, heads), ("x", "z", "core", "head"))
    dp = ("x", "z", "core")
    columns, stacked = P(dp, "head"), P(dp, None, "head")
    in_specs = (columns,) * 5 + (stacked,) * 5 + (P(dp), P(), P())
    out_specs = (columns,) * 3 + (stacked,) * 3 + (P(), P())
    return jax.shard_map(
        per_device, mesh=mesh, in_specs=in_specs, out_specs=out_specs, check_vma=False
    )
```

```python
import functools
import math

import jax
import jax.numpy as jnp
from jax import lax
from jax.experimental import pallas as pl
from jax.experimental.pallas import tpu as pltpu
from jax.sharding import Mesh
from jax.sharding import PartitionSpec as P

NX, NZ, NC = 4, 8, 2
HD = 128
GROUPS = 8
ROWS = 64
PCOLS = GROUPS * ROWS
COLS = 2 * PCOLS
BLOCKS = NX * NZ * NC
KEYS = BLOCKS * ROWS
HALF = KEYS // 2
CHUNK = NZ * ROWS
CG = 256
EXTRA = 8
TAIL = 16
INTERPRET = False
epsilon = 1e-06
masked_value = -1e30
SCALING = 1.0 / math.sqrt(HD)
EXP_SCALE = SCALING * math.log2(math.e)


def unit_rows(values):
    inverse = lax.rsqrt(jnp.mean(values * values, axis=-1, keepdims=True) + epsilon)
    return values * inverse, inverse


def norm_back(unit, inverse, grads, gain):
    scaled = grads * gain
    return inverse * (scaled - unit * jnp.mean(unit * scaled, axis=-1, keepdims=True))


def mm(left, right):
    return jnp.dot(left, right, preferred_element_type=jnp.float32)


def two_heads(ref, pair):
    first = ref[:, 2 * pair * HD : (2 * pair + 1) * HD]
    second = ref[:, (2 * pair + 1) * HD : (2 * pair + 2) * HD]
    return jnp.concatenate([first.astype(jnp.float32), second.astype(jnp.float32)], axis=0)


def prepare_kernel(
    pq_in, pg_in, po_in, rq_in, rg_in, ro_in, gain_in, qn, qn_t, gr, gr_t, delta, held, qgain, sems
):
    f32, bf16 = jnp.float32, jnp.bfloat16
    copies = [
        pltpu.make_async_copy(ref, held.at[i], sems.at[i])
        for i, ref in enumerate((pq_in, rq_in, pg_in, rg_in, po_in, ro_in))
    ]
    copies.append(pltpu.make_async_copy(gain_in, qgain, sems.at[len(copies)]))
    for copy in copies:
        copy.start()
    for copy in copies:
        copy.wait()
    gain_q = qgain[...]
    for part in range(2):
        q, g, o = held.at[part], held.at[2 + part], held.at[4 + part]
        for pair in range(GROUPS // 2):
            r0 = part * PCOLS + pair * 2 * ROWS
            rows = slice(r0, r0 + 2 * ROWS)
            unit, _ = unit_rows(two_heads(q, pair))
            normed = (unit * gain_q).astype(bf16)
            qn[rows, :] = normed
            qn_t[:, rows] = normed.astype(f32).T.astype(bf16)
            grads = two_heads(g, pair)
            gr[rows, :] = grads.astype(bf16)
            gr_t[:, rows] = grads.T.astype(bf16)
            product = grads * two_heads(o, pair)
            delta[:, rows] = jnp.sum(product.T, axis=0, keepdims=True)


def prepare(arrays, qgain):
    f32, bf16 = jnp.float32, jnp.bfloat16
    vmem = pl.BlockSpec(memory_space=pltpu.VMEM)
    out_shape = (
        jax.ShapeDtypeStruct((COLS, HD), bf16),
        jax.ShapeDtypeStruct((HD, COLS), bf16),
        jax.ShapeDtypeStruct((COLS, HD), bf16),
        jax.ShapeDtypeStruct((HD, COLS), bf16),
        jax.ShapeDtypeStruct((1, COLS), f32),
    )
    return pl.pallas_call(
        prepare_kernel,
        out_shape=out_shape,
        in_specs=[pl.BlockSpec(memory_space=pl.ANY)] * (len(arrays) + 1),
        out_specs=tuple([vmem] * len(out_shape)),
        scratch_shapes=[
            pltpu.VMEM((len(arrays), ROWS, GROUPS * HD), bf16),
            pltpu.VMEM((1, HD), f32),
            pltpu.SemaphoreType.DMA((len(arrays) + 1,)),
        ],
        compiler_params=pltpu.CompilerParams(vmem_limit_bytes=56 * 1024 * 1024),
        cost_estimate=pl.CostEstimate(flops=COLS * HD * 40, bytes_accessed=2 << 20, transcendentals=0),
        interpret=INTERPRET,
    )(*arrays, qgain)


def attention_kernel(
    info, own_in, other_in, kgain_in, rk_in, rv_in, qn_in, qn_t_in, gr_in, gr_t_in, delta_in, qgain_in,
    pq_in, rq_in, keep, send, terms, pdq, rdq, rdk, rdv,
    kn, kn_t, vals, kunit, rkn, rkn_t, probs, rprobs, maxima, top, total, factor, dq_t, held, rk, rv,
    weights_b, dscores_b, qn, qn_t, gr, gr_t, delta, qgain, kgain, kv_own, kv_other, sems,
):
    f32, bf16 = jnp.float32, jnp.bfloat16
    kv_refs = (kv_own, kv_other)
    moves = (
        (own_in, kv_own),
        (other_in, kv_other),
        (kgain_in, kgain),
        (rk_in, rk),
        (rv_in, rv),
        (qn_in, qn),
        (qn_t_in, qn_t),
        (gr_in, gr),
        (gr_t_in, gr_t),
        (delta_in, delta),
        (qgain_in, qgain),
        (pq_in, held.at[0]),
        (rq_in, held.at[1]),
    )
    copies = [pltpu.make_async_copy(src, dst, sems.at[i]) for i, (src, dst) in enumerate(moves)]
    for copy in copies:
        copy.start()
    for copy in copies[:3]:
        copy.wait()
    gain_k = kgain[...]

    k0 = 0
    for ref in kv_refs:
        for at in range(0, ref.shape[0], CHUNK):
            rows = slice(k0, k0 + CHUNK)
            unit, _ = unit_rows(ref[at : at + CHUNK, :HD].astype(f32))
            normed = (unit * gain_k).astype(bf16)
            kunit[rows, :] = unit
            kn[rows, :] = normed
            kn_t[k0 // CHUNK] = normed.astype(f32).T.astype(bf16)
            vals[rows, :] = ref[at : at + CHUNK, HD:]
            k0 += CHUNK

    for copy in copies[3:]:
        copy.wait()
    gain_q = qgain[...]
    runit, rinv = unit_rows(rk[...].astype(f32))
    rnormed = (runit * gain_k).astype(bf16)
    rkn[...] = rnormed
    rkn_t[...] = rnormed.astype(f32).T.astype(bf16)

    scores = mm(rkn[...], qn_t[:, PCOLS:]) * EXP_SCALE
    key_at = lax.broadcasted_iota(jnp.int32, (ROWS, PCOLS), 0)
    query_at = lax.broadcasted_iota(jnp.int32, (ROWS, PCOLS), 1) & (ROWS - 1)
    scores = jnp.where(key_at <= query_at, scores, masked_value)
    first = jnp.max(scores, axis=0, keepdims=True)
    raised = jnp.exp2(scores - first)
    rprobs[...] = raised
    rfirst = first
    top[:, :PCOLS] = jnp.full((1, PCOLS), masked_value, f32)
    total[:, :PCOLS] = jnp.zeros((1, PCOLS), f32)
    top[:, PCOLS:] = first
    total[:, PCOLS:] = jnp.sum(raised, axis=0, keepdims=True)

    my_x, my_z, my_core = info[1], info[2], info[3]

    def first_pass(j, _):
        at = pl.multiple_of(j * CHUNK, CHUNK)
        key_x = lax.rem(j, NX)
        key_core = jnp.where(j < NX, my_core, 1 - my_core)

        def tile(c0, masked):
            cols = slice(c0, c0 + CG)
            scores = mm(kn[pl.ds(at, CHUNK), :], qn_t[:, cols]) * EXP_SCALE
            if masked:
                row = lax.broadcasted_iota(jnp.int32, (CHUNK, 1), 0)
                key_block = (key_x * NZ + row // ROWS) * NC + key_core
                key_pos = key_block * ROWS + (row & (ROWS - 1))
                query_pos = lax.broadcasted_iota(jnp.int32, (1, CG), 1) & (ROWS - 1)
                query_pos = query_pos + ((my_x * NZ + my_z) * NC + my_core) * ROWS
                scores = jnp.where(key_pos <= query_pos, scores, masked_value)
            old = top[:, cols]
            new = jnp.maximum(old, jnp.max(scores, axis=0, keepdims=True))
            raised = jnp.exp2(scores - new)
            probs[pl.ds(at, CHUNK), cols] = raised
            total[:, cols] = total[:, cols] * jnp.exp2(old - new) + jnp.sum(
                raised, axis=0, keepdims=True
            )
            top[:, cols] = new
            maxima[j, :, cols] = new

        @pl.when(key_x < my_x)
        def _():
            for c0 in range(0, COLS, CG):
                tile(c0, False)

        @pl.when(key_x >= my_x)
        def _():
            for c0 in range(0, COLS, CG):
                tile(c0, c0 < PCOLS)

        return 0

    lax.fori_loop(0, KEYS // CHUNK, first_pass, 0)

    column = lax.broadcasted_iota(jnp.int32, (1, COLS), 1)
    living = (column < PCOLS) | ((column & (ROWS - 1)) < info[0])
    factor[...] = jnp.where(living, 1.0 / total[...], 0.0)
    dq_t[...] = jnp.zeros_like(dq_t)

    def second_pass(out, base, j, carry):
        key_terms, largest_k, largest_v = carry
        at = pl.multiple_of(j * CHUNK, CHUNK)
        here = pl.multiple_of((j - base) * CHUNK, CHUNK)
        values = vals[pl.ds(at, CHUNK), :]
        keys_t = kn_t[j]
        for c0 in range(0, COLS, CG):
            cols = slice(c0, c0 + CG)
            scale = jnp.exp2(maxima[j, :, cols] - top[:, cols]) * factor[:, cols]
            weights = probs[pl.ds(at, CHUNK), cols] * scale
            dweights = mm(values, gr_t[:, cols])
            weights_b[:, cols] = weights.astype(bf16)
            dscores_b[:, cols] = (weights * (dweights - delta[:, cols])).astype(bf16)
        dvalue = mm(weights_b[...], gr[...])
        dkey = mm(dscores_b[...], qn[...])
        dq_t[...] = dq_t[...] + mm(keys_t, dscores_b[...])
        dkey = dkey * SCALING
        out[pl.ds(here, CHUNK), :HD] = dkey
        out[pl.ds(here, CHUNK), HD:] = dvalue
        products = dkey * kunit[pl.ds(at, CHUNK), :]
        eights = (CHUNK // 8, 8, HD)
        return (
            key_terms + jnp.sum(products.reshape(eights), axis=0),
            jnp.maximum(largest_k, jnp.max(jnp.abs(dkey).reshape(eights), axis=0)),
            jnp.maximum(largest_v, jnp.max(jnp.abs(dvalue).reshape(eights), axis=0)),
        )

    half = HALF // CHUNK
    zero = jnp.zeros((8, HD), f32)
    key_terms = zero
    for out, base in ((send, half), (keep, 0)):
        key_terms, largest_k, largest_v = lax.fori_loop(
            base, base + half, functools.partial(second_pass, out, base), (key_terms, zero, zero)
        )
        out[HALF:, :HD] = jnp.broadcast_to(jnp.max(largest_k, axis=0, keepdims=True), (EXTRA, HD))
        out[HALF:, HD:] = jnp.broadcast_to(jnp.max(largest_v, axis=0, keepdims=True), (EXTRA, HD))

    right = slice(PCOLS, COLS)
    scale = jnp.exp2(rfirst - top[:, right]) * factor[:, right]
    weights = rprobs[...] * scale
    dweights = mm(rv[...], gr_t[:, right])
    dscores = (weights * (dweights - delta[:, right])).astype(bf16)
    rdv[...] = mm(weights.astype(bf16), gr[right, :]).astype(bf16)
    dkey = mm(dscores, qn[right, :]) * SCALING
    rdk[...] = norm_back(runit, rinv, dkey, gain_k).astype(bf16)
    dq_t[:, right] = dq_t[:, right] + mm(rkn_t[...], dscores)
    key_terms = jnp.sum(key_terms, axis=0, keepdims=True)
    key_terms = key_terms + jnp.sum(dkey * runit, axis=0, keepdims=True)

    query_terms = jnp.zeros((1, HD), f32)
    for part, out in enumerate((pdq, rdq)):
        q = held.at[part]
        for pair in range(GROUPS // 2):
            r0 = part * PCOLS + pair * 2 * ROWS
            unit, inverse = unit_rows(two_heads(q, pair))
            dquery = dq_t[:, r0 : r0 + 2 * ROWS].T * SCALING
            query_terms = query_terms + jnp.sum(dquery * unit, axis=0, keepdims=True)
            raw = norm_back(unit, inverse, dquery, gain_q).astype(bf16)
            out[:, 2 * pair * HD : (2 * pair + 1) * HD] = raw[:ROWS]
            out[:, (2 * pair + 1) * HD : (2 * pair + 2) * HD] = raw[ROWS:]

    terms[:, :HD] = jnp.broadcast_to(query_terms, (EXTRA, HD))
    terms[:, HD:] = jnp.broadcast_to(key_terms, (EXTRA, HD))


def attention(info, arrays):
    f32, bf16 = jnp.float32, jnp.bfloat16
    vmem = pl.BlockSpec(memory_space=pltpu.VMEM)
    smem = pl.BlockSpec(memory_space=pltpu.SMEM)
    out_shape = (
        jax.ShapeDtypeStruct((HALF + EXTRA, 2 * HD), f32),
        jax.ShapeDtypeStruct((HALF + EXTRA, 2 * HD), f32),
        jax.ShapeDtypeStruct((EXTRA, 2 * HD), f32),
        jax.ShapeDtypeStruct((ROWS, GROUPS * HD), bf16),
        jax.ShapeDtypeStruct((ROWS, GROUPS * HD), bf16),
        jax.ShapeDtypeStruct((ROWS, HD), bf16),
        jax.ShapeDtypeStruct((ROWS, HD), bf16),
    )
    chunks = KEYS // CHUNK
    scratch = [
        pltpu.VMEM((KEYS, HD), bf16),
        pltpu.VMEM((chunks, HD, CHUNK), bf16),
        pltpu.VMEM((KEYS, HD), bf16),
        pltpu.VMEM((KEYS, HD), f32),
        pltpu.VMEM((ROWS, HD), bf16),
        pltpu.VMEM((HD, ROWS), bf16),
        pltpu.VMEM((KEYS, COLS), f32),
        pltpu.VMEM((ROWS, PCOLS), f32),
        pltpu.VMEM((chunks, 1, COLS), f32),
        pltpu.VMEM((1, COLS), f32),
        pltpu.VMEM((1, COLS), f32),
        pltpu.VMEM((1, COLS), f32),
        pltpu.VMEM((HD, COLS), f32),
        pltpu.VMEM((2, ROWS, GROUPS * HD), bf16),
        pltpu.VMEM((ROWS, HD), bf16),
        pltpu.VMEM((ROWS, HD), bf16),
        pltpu.VMEM((CHUNK, COLS), bf16),
        pltpu.VMEM((CHUNK, COLS), bf16),
        pltpu.VMEM((COLS, HD), bf16),
        pltpu.VMEM((HD, COLS), bf16),
        pltpu.VMEM((COLS, HD), bf16),
        pltpu.VMEM((HD, COLS), bf16),
        pltpu.VMEM((1, COLS), f32),
        pltpu.VMEM((1, HD), f32),
        pltpu.VMEM((1, HD), f32),
        pltpu.VMEM((HALF, 2 * HD), bf16),
        pltpu.VMEM((HALF, 2 * HD), bf16),
        pltpu.SemaphoreType.DMA((len(arrays),)),
    ]
    return pl.pallas_call(
        attention_kernel,
        out_shape=out_shape,
        in_specs=[smem] + [pl.BlockSpec(memory_space=pl.ANY)] * len(arrays),
        out_specs=tuple([vmem] * len(out_shape)),
        scratch_shapes=scratch,
        compiler_params=pltpu.CompilerParams(vmem_limit_bytes=56 * 1024 * 1024),
        cost_estimate=pl.CostEstimate(
            flops=10 * KEYS * COLS * HD, bytes_accessed=8 << 20, transcendentals=KEYS * COLS
        ),
        interpret=INTERPRET,
    )(info, *arrays)


def exchange(array, axis):
    return lax.all_to_all(array, axis, 0, 0, tiled=True)


def exchange_halves(message, axis):
    halves = message.astype(jnp.float16).reshape(-1, 2 * HD)
    return exchange(halves, axis).astype(jnp.float32).reshape(message.shape)


def swap_core(array):
    return lax.ppermute(array, "core", [(0, 1), (1, 0)])


def pack_message(message, rows, count, blocks, largest, terms):
    exponent = jnp.clip(jnp.floor(jnp.log2(jnp.maximum(largest, 1e-37))), -100.0, 100.0)
    scale = jnp.exp2(14.0 - exponent)
    term_exponent = jnp.clip(
        jnp.floor(jnp.log2(jnp.maximum(jnp.abs(terms), 1e-37))), -100.0, 100.0
    )
    scaled = terms * jnp.exp2(14.0 - term_exponent)
    high = scaled.astype(jnp.bfloat16).astype(jnp.float32)
    low = (scaled - high) * 256.0
    row = lax.broadcasted_iota(jnp.int32, (TAIL, 2 * HD), 0)
    tail = jnp.where(row == 2, exponent, term_exponent)
    tail = jnp.where(row == 0, high, jnp.where(row == 1, low, tail))
    for i in range(count):
        message[i, :rows] = blocks(i) * scale
        message[i, rows:] = tail


def unpack_message(message, rows, count):
    total = jnp.zeros((rows, 2 * HD), jnp.float32)
    terms = jnp.zeros((1, 2 * HD), jnp.float32)
    for i in range(count):
        tail = message[i, rows:]
        total = total + message[i, :rows] * jnp.exp2(tail[2:3] - 14.0)
        terms = terms + (tail[0:1] + tail[1:2] * (1.0 / 256.0)) * jnp.exp2(tail[3:4] - 14.0)
    return total, terms


def first_stage_kernel(keep, got, message):
    rows = NZ * ROWS
    largest = keep[HALF : HALF + 1, :] + got[HALF : HALF + 1, :]

    def blocks(i):
        return keep[i * rows : (i + 1) * rows, :] + got[i * rows : (i + 1) * rows, :]

    pack_message(message, rows, NX, blocks, largest, jnp.zeros((1, 2 * HD), jnp.float32))


def second_stage_kernel(got, all_terms, message):
    total, _ = unpack_message(got, NZ * ROWS, NX)
    row = lax.broadcasted_iota(jnp.int32, all_terms.shape, 0) & (EXTRA - 1)
    terms = jnp.sum(jnp.where(row == 0, all_terms[...], 0.0), axis=0, keepdims=True)
    largest = jnp.max(jnp.abs(total), axis=0, keepdims=True)
    pack_message(message, ROWS, NZ, lambda i: total[i * ROWS : (i + 1) * ROWS], largest, terms)


def last_stage_kernel(got, keys, kgain, pdk, pdv, query_terms, key_terms):
    total, terms = unpack_message(got, ROWS, NZ)
    unit, inverse = unit_rows(keys[...].astype(jnp.float32))
    pdk[...] = norm_back(unit, inverse, total[:, :HD], kgain[...]).astype(jnp.bfloat16)
    pdv[...] = total[:, HD:].astype(jnp.bfloat16)
    query_terms[...] = terms[:, :HD]
    key_terms[...] = terms[:, HD:]


def small_kernel(body, out_shape, *arrays):
    vmem = pl.BlockSpec(memory_space=pltpu.VMEM)
    outs = vmem if isinstance(out_shape, jax.ShapeDtypeStruct) else tuple([vmem] * len(out_shape))
    return pl.pallas_call(
        body,
        out_shape=out_shape,
        in_specs=[vmem] * len(arrays),
        out_specs=outs,
        compiler_params=pltpu.CompilerParams(vmem_limit_bytes=16 * 1024 * 1024),
        cost_estimate=pl.CostEstimate(flops=1 << 20, bytes_accessed=4 << 20, transcendentals=0),
        interpret=INTERPRET,
    )(*arrays)


def per_device(
    prompt_query,
    prompt_key,
    prompt_value,
    prompt_out,
    prompt_grad,
    response_query,
    response_key,
    response_value,
    response_out,
    response_grad,
    lengths,
    query_gain,
    key_gain,
):
    place = [lax.axis_index(name).astype(jnp.int32)[None] for name in ("x", "z", "core")]
    info = jnp.concatenate([lengths, *place])
    qgain, kgain = query_gain.reshape(1, HD), key_gain.reshape(1, HD)

    local = jnp.concatenate([prompt_key, prompt_value], axis=1)
    own = lax.all_gather(lax.all_gather(local, "z", axis=0, tiled=True), "x", axis=0, tiled=True)
    raw = [prompt_query, prompt_grad, prompt_out, response_query[0], response_grad[0], response_out[0]]
    prepared = prepare(raw, qgain)
    own, prepared = lax.optimization_barrier((own, prepared))
    other = swap_core(own)
    keep, give, terms, pdq, rdq, rdk, rdv = attention(
        info,
        [
            own,
            other,
            kgain,
            response_key[0],
            response_value[0],
            *prepared,
            qgain,
            prompt_query,
            response_query[0],
        ],
    )

    got = swap_core(give)
    terms = jnp.sum(lax.all_gather(terms, "head", axis=0), axis=0)
    terms = lax.all_gather(terms, ("x", "core"), axis=0, tiled=True)
    rows = NZ * ROWS + TAIL
    message = small_kernel(
        first_stage_kernel, jax.ShapeDtypeStruct((NX, rows, 2 * HD), jnp.float32), keep, got
    )
    message = exchange_halves(message, "x")
    rows = ROWS + TAIL
    message = small_kernel(
        second_stage_kernel, jax.ShapeDtypeStruct((NZ, rows, 2 * HD), jnp.float32), message, terms
    )
    message = exchange_halves(message, "z")
    block = jax.ShapeDtypeStruct((ROWS, HD), jnp.bfloat16)
    gain = jax.ShapeDtypeStruct((1, HD), jnp.float32)
    pdk, pdv, query_total, key_total = small_kernel(
        last_stage_kernel, (block, block, gain, gain), message, prompt_key, kgain
    )
    return pdq, pdk, pdv, rdq[None], rdk[None], rdv[None], query_total[0], key_total[0]


def solution(mesh):
    heads = mesh.devices.shape[1]
    mesh = Mesh(mesh.devices.reshape(NX, NZ, NC, heads), ("x", "z", "core", "head"))
    dp = ("x", "z", "core")
    columns, stacked = P(dp, "head"), P(dp, None, "head")
    in_specs = (columns,) * 5 + (stacked,) * 5 + (P(dp), P(), P())
    out_specs = (columns,) * 3 + (stacked,) * 3 + (P(), P())
    return jax.shard_map(
        per_device, mesh=mesh, in_specs=in_specs, out_specs=out_specs, check_vma=False
    )
```

```python
import functools
import math

import jax
import jax.numpy as jnp
from jax import lax
from jax.experimental import pallas as pl
from jax.experimental.pallas import tpu as pltpu
from jax.sharding import Mesh
from jax.sharding import PartitionSpec as P

NX, NZ, NC = 4, 8, 2
HD = 128
GROUPS = 8
ROWS = 64
PCOLS = GROUPS * ROWS
COLS = 2 * PCOLS
BLOCKS = NX * NZ * NC
KEYS = BLOCKS * ROWS
HALF = KEYS // 2
CHUNK = NZ * ROWS
CG = 256
EXTRA = 8
TAIL = 16
INTERPRET = False
epsilon = 1e-06
masked_value = -1e30
SCALING = 1.0 / math.sqrt(HD)
EXP_SCALE = SCALING * math.log2(math.e)


def unit_rows(values):
    inverse = lax.rsqrt(jnp.mean(values * values, axis=-1, keepdims=True) + epsilon)
    return values * inverse, inverse


def norm_back(unit, inverse, grads, gain):
    scaled = grads * gain
    return inverse * (scaled - unit * jnp.mean(unit * scaled, axis=-1, keepdims=True))


def mm(left, right):
    return jnp.dot(left, right, preferred_element_type=jnp.float32)


def two_heads(ref, pair):
    first = ref[:, 2 * pair * HD : (2 * pair + 1) * HD]
    second = ref[:, (2 * pair + 1) * HD : (2 * pair + 2) * HD]
    return jnp.concatenate([first.astype(jnp.float32), second.astype(jnp.float32)], axis=0)


def prepare_kernel(
    pq_in, pg_in, po_in, rq_in, rg_in, ro_in, gain_in, qn, qn_t, gr, gr_t, delta, held, qgain, sems
):
    f32, bf16 = jnp.float32, jnp.bfloat16
    copies = [
        pltpu.make_async_copy(ref, held.at[i], sems.at[i])
        for i, ref in enumerate((pq_in, rq_in, pg_in, rg_in, po_in, ro_in))
    ]
    copies.append(pltpu.make_async_copy(gain_in, qgain, sems.at[len(copies)]))
    for copy in copies:
        copy.start()
    for copy in copies:
        copy.wait()
    gain_q = qgain[...]
    for part in range(2):
        q, g, o = held.at[part], held.at[2 + part], held.at[4 + part]
        for pair in range(GROUPS // 2):
            r0 = part * PCOLS + pair * 2 * ROWS
            rows = slice(r0, r0 + 2 * ROWS)
            unit, _ = unit_rows(two_heads(q, pair))
            normed = (unit * gain_q).astype(bf16)
            qn[rows, :] = normed
            qn_t[:, rows] = normed.astype(f32).T.astype(bf16)
            grads = two_heads(g, pair)
            gr[rows, :] = grads.astype(bf16)
            gr_t[:, rows] = grads.T.astype(bf16)
            product = grads * two_heads(o, pair)
            delta[:, rows] = jnp.sum(product.T, axis=0, keepdims=True)


def prepare(arrays, qgain):
    f32, bf16 = jnp.float32, jnp.bfloat16
    vmem = pl.BlockSpec(memory_space=pltpu.VMEM)
    out_shape = (
        jax.ShapeDtypeStruct((COLS, HD), bf16),
        jax.ShapeDtypeStruct((HD, COLS), bf16),
        jax.ShapeDtypeStruct((COLS, HD), bf16),
        jax.ShapeDtypeStruct((HD, COLS), bf16),
        jax.ShapeDtypeStruct((1, COLS), f32),
    )
    return pl.pallas_call(
        prepare_kernel,
        out_shape=out_shape,
        in_specs=[pl.BlockSpec(memory_space=pl.ANY)] * (len(arrays) + 1),
        out_specs=tuple([vmem] * len(out_shape)),
        scratch_shapes=[
            pltpu.VMEM((len(arrays), ROWS, GROUPS * HD), bf16),
            pltpu.VMEM((1, HD), f32),
            pltpu.SemaphoreType.DMA((len(arrays) + 1,)),
        ],
        compiler_params=pltpu.CompilerParams(vmem_limit_bytes=8 * 1024 * 1024),
        cost_estimate=pl.CostEstimate(flops=COLS * HD * 40, bytes_accessed=2 << 20, transcendentals=0),
        interpret=INTERPRET,
    )(*arrays, qgain)


def attention_kernel(
    info, own_in, other_in, kgain_in, rk_in, rv_in, qn_in, qn_t_in, gr_in, gr_t_in, delta_in, qgain_in,
    pq_in, rq_in, keep, send, pdq, rdq, rdk, rdv,
    kn, kn_t, vals, kunit, rkn, rkn_t, probs, rprobs, maxima, top, total, factor, dq_t, held, rk, rv,
    weights_b, dscores_b, qn, qn_t, gr, gr_t, delta, qgain, kgain, kv_own, kv_other, sems,
):
    f32, bf16 = jnp.float32, jnp.bfloat16
    kv_refs = (kv_own, kv_other)
    moves = (
        (own_in, kv_own),
        (other_in, kv_other),
        (kgain_in, kgain),
        (rk_in, rk),
        (rv_in, rv),
        (qn_in, qn),
        (qn_t_in, qn_t),
        (gr_in, gr),
        (gr_t_in, gr_t),
        (delta_in, delta),
        (qgain_in, qgain),
        (pq_in, held.at[0]),
        (rq_in, held.at[1]),
    )
    copies = [pltpu.make_async_copy(src, dst, sems.at[i]) for i, (src, dst) in enumerate(moves)]
    for copy in copies:
        copy.start()
    for copy in copies[:3]:
        copy.wait()
    gain_k = kgain[...]

    k0 = 0
    for ref in kv_refs:
        for at in range(0, ref.shape[0], CHUNK):
            rows = slice(k0, k0 + CHUNK)
            unit, _ = unit_rows(ref[at : at + CHUNK, :HD].astype(f32))
            normed = (unit * gain_k).astype(bf16)
            kunit[rows, :] = unit
            kn[rows, :] = normed
            kn_t[k0 // CHUNK] = normed.astype(f32).T.astype(bf16)
            vals[rows, :] = ref[at : at + CHUNK, HD:]
            k0 += CHUNK

    for copy in copies[3:]:
        copy.wait()
    gain_q = qgain[...]
    runit, rinv = unit_rows(rk[...].astype(f32))
    rnormed = (runit * gain_k).astype(bf16)
    rkn[...] = rnormed
    rkn_t[...] = rnormed.astype(f32).T.astype(bf16)

    scores = mm(rkn[...], qn_t[:, PCOLS:]) * EXP_SCALE
    key_at = lax.broadcasted_iota(jnp.int32, (ROWS, PCOLS), 0)
    query_at = lax.broadcasted_iota(jnp.int32, (ROWS, PCOLS), 1) & (ROWS - 1)
    scores = jnp.where(key_at <= query_at, scores, masked_value)
    first = jnp.max(scores, axis=0, keepdims=True)
    raised = jnp.exp2(scores - first)
    rprobs[...] = raised
    rfirst = first
    top[:, :PCOLS] = jnp.full((1, PCOLS), masked_value, f32)
    total[:, :PCOLS] = jnp.zeros((1, PCOLS), f32)
    top[:, PCOLS:] = first
    total[:, PCOLS:] = jnp.sum(raised, axis=0, keepdims=True)

    my_x, my_z, my_core = info[1], info[2], info[3]

    def first_pass(j, _):
        at = pl.multiple_of(j * CHUNK, CHUNK)
        key_x = lax.rem(j, NX)
        key_core = jnp.where(j < NX, my_core, 1 - my_core)

        def tile(c0, masked):
            cols = slice(c0, c0 + CG)
            scores = mm(kn[pl.ds(at, CHUNK), :], qn_t[:, cols]) * EXP_SCALE
            if masked:
                row = lax.broadcasted_iota(jnp.int32, (CHUNK, 1), 0)
                key_block = (key_x * NZ + row // ROWS) * NC + key_core
                key_pos = key_block * ROWS + (row & (ROWS - 1))
                query_pos = lax.broadcasted_iota(jnp.int32, (1, CG), 1) & (ROWS - 1)
                query_pos = query_pos + ((my_x * NZ + my_z) * NC + my_core) * ROWS
                scores = jnp.where(key_pos <= query_pos, scores, masked_value)
            old = top[:, cols]
            new = jnp.maximum(old, jnp.max(scores, axis=0, keepdims=True))
            raised = jnp.exp2(scores - new)
            probs[pl.ds(at, CHUNK), cols] = raised
            total[:, cols] = total[:, cols] * jnp.exp2(old - new) + jnp.sum(
                raised, axis=0, keepdims=True
            )
            top[:, cols] = new
            maxima[j, :, cols] = new

        @pl.when(key_x < my_x)
        def _():
            for c0 in range(0, COLS, CG):
                tile(c0, False)

        @pl.when(key_x >= my_x)
        def _():
            for c0 in range(0, COLS, CG):
                tile(c0, c0 < PCOLS)

        return 0

    lax.fori_loop(0, KEYS // CHUNK, first_pass, 0)

    column = lax.broadcasted_iota(jnp.int32, (1, COLS), 1)
    living = (column < PCOLS) | ((column & (ROWS - 1)) < info[0])
    factor[...] = jnp.where(living, 1.0 / total[...], 0.0)
    dq_t[...] = jnp.zeros_like(dq_t)

    def second_pass(out, base, j, carry):
        key_terms, largest_k, largest_v = carry
        at = pl.multiple_of(j * CHUNK, CHUNK)
        here = pl.multiple_of((j - base) * CHUNK, CHUNK)
        values = vals[pl.ds(at, CHUNK), :]
        keys_t = kn_t[j]
        for c0 in range(0, COLS, CG):
            cols = slice(c0, c0 + CG)
            scale = jnp.exp2(maxima[j, :, cols] - top[:, cols]) * factor[:, cols]
            weights = probs[pl.ds(at, CHUNK), cols] * scale
            dweights = mm(values, gr_t[:, cols])
            weights_b[:, cols] = weights.astype(bf16)
            dscores_b[:, cols] = (weights * (dweights - delta[:, cols])).astype(bf16)
        dvalue = mm(weights_b[...], gr[...])
        dkey = mm(dscores_b[...], qn[...])
        dq_t[...] = dq_t[...] + mm(keys_t, dscores_b[...])
        dkey = dkey * SCALING
        out[pl.ds(here, CHUNK), :HD] = dkey
        out[pl.ds(here, CHUNK), HD:] = dvalue
        products = dkey * kunit[pl.ds(at, CHUNK), :]
        eights = (CHUNK // 8, 8, HD)
        return (
            key_terms + jnp.sum(products.reshape(eights), axis=0),
            jnp.maximum(largest_k, jnp.max(jnp.abs(dkey).reshape(eights), axis=0)),
            jnp.maximum(largest_v, jnp.max(jnp.abs(dvalue).reshape(eights), axis=0)),
        )

    half = HALF // CHUNK
    zero = jnp.zeros((8, HD), f32)
    key_terms = zero
    for out, base in ((send, half), (keep, 0)):
        key_terms, largest_k, largest_v = lax.fori_loop(
            base, base + half, functools.partial(second_pass, out, base), (key_terms, zero, zero)
        )
        out[HALF:, :HD] = jnp.broadcast_to(jnp.max(largest_k, axis=0, keepdims=True), (EXTRA, HD))
        out[HALF:, HD:] = jnp.broadcast_to(jnp.max(largest_v, axis=0, keepdims=True), (EXTRA, HD))

    right = slice(PCOLS, COLS)
    scale = jnp.exp2(rfirst - top[:, right]) * factor[:, right]
    weights = rprobs[...] * scale
    dweights = mm(rv[...], gr_t[:, right])
    dscores = (weights * (dweights - delta[:, right])).astype(bf16)
    rdv[...] = mm(weights.astype(bf16), gr[right, :]).astype(bf16)
    dkey = mm(dscores, qn[right, :]) * SCALING
    rdk[...] = norm_back(runit, rinv, dkey, gain_k).astype(bf16)
    dq_t[:, right] = dq_t[:, right] + mm(rkn_t[...], dscores)
    key_terms = jnp.sum(key_terms, axis=0, keepdims=True)
    key_terms = key_terms + jnp.sum(dkey * runit, axis=0, keepdims=True)

    query_terms = jnp.zeros((1, HD), f32)
    for part, out in enumerate((pdq, rdq)):
        q = held.at[part]
        for pair in range(GROUPS // 2):
            r0 = part * PCOLS + pair * 2 * ROWS
            unit, inverse = unit_rows(two_heads(q, pair))
            dquery = dq_t[:, r0 : r0 + 2 * ROWS].T * SCALING
            query_terms = query_terms + jnp.sum(dquery * unit, axis=0, keepdims=True)
            raw = norm_back(unit, inverse, dquery, gain_q).astype(bf16)
            out[:, 2 * pair * HD : (2 * pair + 1) * HD] = raw[:ROWS]
            out[:, (2 * pair + 1) * HD : (2 * pair + 2) * HD] = raw[ROWS:]

    for out in (keep, send):
        out[HALF + 1 : HALF + 2, :HD] = query_terms
        out[HALF + 1 : HALF + 2, HD:] = key_terms


def attention(info, arrays):
    f32, bf16 = jnp.float32, jnp.bfloat16
    vmem = pl.BlockSpec(memory_space=pltpu.VMEM)
    smem = pl.BlockSpec(memory_space=pltpu.SMEM)
    out_shape = (
        jax.ShapeDtypeStruct((HALF + EXTRA, 2 * HD), f32),
        jax.ShapeDtypeStruct((HALF + EXTRA, 2 * HD), f32),
        jax.ShapeDtypeStruct((ROWS, GROUPS * HD), bf16),
        jax.ShapeDtypeStruct((ROWS, GROUPS * HD), bf16),
        jax.ShapeDtypeStruct((ROWS, HD), bf16),
        jax.ShapeDtypeStruct((ROWS, HD), bf16),
    )
    chunks = KEYS // CHUNK
    scratch = [
        pltpu.VMEM((KEYS, HD), bf16),
        pltpu.VMEM((chunks, HD, CHUNK), bf16),
        pltpu.VMEM((KEYS, HD), bf16),
        pltpu.VMEM((KEYS, HD), f32),
        pltpu.VMEM((ROWS, HD), bf16),
        pltpu.VMEM((HD, ROWS), bf16),
        pltpu.VMEM((KEYS, COLS), f32),
        pltpu.VMEM((ROWS, PCOLS), f32),
        pltpu.VMEM((chunks, 1, COLS), f32),
        pltpu.VMEM((1, COLS), f32),
        pltpu.VMEM((1, COLS), f32),
        pltpu.VMEM((1, COLS), f32),
        pltpu.VMEM((HD, COLS), f32),
        pltpu.VMEM((2, ROWS, GROUPS * HD), bf16),
        pltpu.VMEM((ROWS, HD), bf16),
        pltpu.VMEM((ROWS, HD), bf16),
        pltpu.VMEM((CHUNK, COLS), bf16),
        pltpu.VMEM((CHUNK, COLS), bf16),
        pltpu.VMEM((COLS, HD), bf16),
        pltpu.VMEM((HD, COLS), bf16),
        pltpu.VMEM((COLS, HD), bf16),
        pltpu.VMEM((HD, COLS), bf16),
        pltpu.VMEM((1, COLS), f32),
        pltpu.VMEM((1, HD), f32),
        pltpu.VMEM((1, HD), f32),
        pltpu.VMEM((HALF, 2 * HD), bf16),
        pltpu.VMEM((HALF, 2 * HD), bf16),
        pltpu.SemaphoreType.DMA((len(arrays),)),
    ]
    return pl.pallas_call(
        attention_kernel,
        out_shape=out_shape,
        in_specs=[smem] + [pl.BlockSpec(memory_space=pl.ANY)] * len(arrays),
        out_specs=tuple([vmem] * len(out_shape)),
        scratch_shapes=scratch,
        compiler_params=pltpu.CompilerParams(vmem_limit_bytes=48 * 1024 * 1024),
        cost_estimate=pl.CostEstimate(
            flops=10 * KEYS * COLS * HD, bytes_accessed=8 << 20, transcendentals=KEYS * COLS
        ),
        interpret=INTERPRET,
    )(info, *arrays)


def exchange(array, axis):
    return lax.all_to_all(array, axis, 0, 0, tiled=True)


def exchange_copies(array, axis):
    count = lax.axis_size(axis)
    copies = jnp.broadcast_to(array[None], (count,) + array.shape)
    return exchange(copies.reshape((-1,) + array.shape[1:]), axis)


def exchange_halves(halves, axis):
    got = exchange(halves.reshape(-1, 2 * HD), axis)
    return got.astype(jnp.float32).reshape(halves.shape)


def swap_core(array):
    return lax.ppermute(array, "core", [(0, 1), (1, 0)])


def pack_message(message, rows, count, blocks, largest, terms):
    exponent = jnp.clip(jnp.floor(jnp.log2(jnp.maximum(largest, 1e-37))), -100.0, 100.0)
    scale = jnp.exp2(14.0 - exponent)
    term_exponent = jnp.clip(
        jnp.floor(jnp.log2(jnp.maximum(jnp.abs(terms), 1e-37))), -100.0, 100.0
    )
    scaled = terms * jnp.exp2(14.0 - term_exponent)
    high = scaled.astype(jnp.bfloat16).astype(jnp.float32)
    low = (scaled - high) * 256.0
    row = lax.broadcasted_iota(jnp.int32, (TAIL, 2 * HD), 0)
    tail = jnp.where(row == 2, exponent, term_exponent)
    tail = jnp.where(row == 0, high, jnp.where(row == 1, low, tail))
    for i in range(count):
        message[i, :rows] = blocks(i) * scale
        message[i, rows:] = tail


def unpack_message(message, rows, count):
    total = jnp.zeros((rows, 2 * HD), jnp.float32)
    terms = jnp.zeros((1, 2 * HD), jnp.float32)
    for i in range(count):
        tail = message[i, rows:]
        total = total + message[i, :rows] * jnp.exp2(tail[2:3] - 14.0)
        terms = terms + (tail[0:1] + tail[1:2] * (1.0 / 256.0)) * jnp.exp2(tail[3:4] - 14.0)
    return total, terms


def first_stage_kernel(keep, got, message, terms):
    rows = NZ * ROWS
    largest = keep[HALF : HALF + 1, :] + got[HALF : HALF + 1, :]

    def blocks(i):
        return keep[i * rows : (i + 1) * rows, :] + got[i * rows : (i + 1) * rows, :]

    terms[...] = jnp.broadcast_to(
        keep[HALF + 1 : HALF + 2, :] + got[HALF + 1 : HALF + 2, :], terms.shape
    )
    pack_message(message, rows, NX, blocks, largest, jnp.zeros((1, 2 * HD), jnp.float32))


def second_stage_kernel(got, all_terms, message):
    total, _ = unpack_message(got, NZ * ROWS, NX)
    row = lax.broadcasted_iota(jnp.int32, all_terms.shape, 0) & (EXTRA - 1)
    terms = jnp.sum(jnp.where(row == 0, all_terms[...], 0.0), axis=0, keepdims=True)
    largest = jnp.max(jnp.abs(total), axis=0, keepdims=True)
    pack_message(message, ROWS, NZ, lambda i: total[i * ROWS : (i + 1) * ROWS], largest, terms)


def last_stage_kernel(got, keys, kgain, pdk, pdv, query_terms, key_terms):
    total, terms = unpack_message(got, ROWS, NZ)
    unit, inverse = unit_rows(keys[...].astype(jnp.float32))
    pdk[...] = norm_back(unit, inverse, total[:, :HD], kgain[...]).astype(jnp.bfloat16)
    pdv[...] = total[:, HD:].astype(jnp.bfloat16)
    query_terms[...] = terms[:, :HD]
    key_terms[...] = terms[:, HD:]


def small_kernel(body, out_shape, *arrays):
    vmem = pl.BlockSpec(memory_space=pltpu.VMEM)
    outs = vmem if isinstance(out_shape, jax.ShapeDtypeStruct) else tuple([vmem] * len(out_shape))
    return pl.pallas_call(
        body,
        out_shape=out_shape,
        in_specs=[vmem] * len(arrays),
        out_specs=outs,
        compiler_params=pltpu.CompilerParams(vmem_limit_bytes=16 * 1024 * 1024),
        cost_estimate=pl.CostEstimate(flops=1 << 20, bytes_accessed=4 << 20, transcendentals=0),
        interpret=INTERPRET,
    )(*arrays)


def per_device(
    prompt_query,
    prompt_key,
    prompt_value,
    prompt_out,
    prompt_grad,
    response_query,
    response_key,
    response_value,
    response_out,
    response_grad,
    lengths,
    query_gain,
    key_gain,
):
    place = [lax.axis_index(name).astype(jnp.int32)[None] for name in ("x", "z", "core")]
    info = jnp.concatenate([lengths, *place])
    qgain, kgain = query_gain.reshape(1, HD), key_gain.reshape(1, HD)

    local = jnp.concatenate([prompt_key, prompt_value], axis=1)
    own = exchange_copies(local, ("x", "z"))
    raw = [prompt_query, prompt_grad, prompt_out, response_query[0], response_grad[0], response_out[0]]
    prepared = prepare(raw, qgain)
    own, prepared = lax.optimization_barrier((own, prepared))
    other = swap_core(own)
    keep, give, pdq, rdq, rdk, rdv = attention(
        info,
        [
            own,
            other,
            kgain,
            response_key[0],
            response_value[0],
            *prepared,
            qgain,
            prompt_query,
            response_query[0],
        ],
    )

    got = swap_core(give)
    rows = NZ * ROWS + TAIL
    message, terms = small_kernel(
        first_stage_kernel,
        (
            jax.ShapeDtypeStruct((NX, rows, 2 * HD), jnp.float32),
            jax.ShapeDtypeStruct((EXTRA, 2 * HD), jnp.float32),
        ),
        keep,
        got,
    )
    halves, terms = lax.optimization_barrier((message.astype(jnp.float16), terms))
    message = exchange_halves(halves, "x")
    terms = exchange_copies(terms, "head").reshape(-1, EXTRA, 2 * HD).sum(axis=0)
    terms = exchange_copies(terms, "x")
    rows = ROWS + TAIL
    message = small_kernel(
        second_stage_kernel, jax.ShapeDtypeStruct((NZ, rows, 2 * HD), jnp.float32), message, terms
    )
    message = exchange_halves(message.astype(jnp.float16), "z")
    block = jax.ShapeDtypeStruct((ROWS, HD), jnp.bfloat16)
    gain = jax.ShapeDtypeStruct((1, HD), jnp.float32)
    pdk, pdv, query_total, key_total = small_kernel(
        last_stage_kernel, (block, block, gain, gain), message, prompt_key, kgain
    )
    return pdq, pdk, pdv, rdq[None], rdk[None], rdv[None], query_total[0], key_total[0]


def solution(mesh):
    heads = mesh.devices.shape[1]
    mesh = Mesh(mesh.devices.reshape(NX, NZ, NC, heads), ("x", "z", "core", "head"))
    dp = ("x", "z", "core")
    columns, stacked = P(dp, "head"), P(dp, None, "head")
    in_specs = (columns,) * 5 + (stacked,) * 5 + (P(dp), P(), P())
    out_specs = (columns,) * 3 + (stacked,) * 3 + (P(), P())
    return jax.shard_map(
        per_device, mesh=mesh, in_specs=in_specs, out_specs=out_specs, check_vma=False
    )
```

```python
import functools
import math

import jax
import jax.numpy as jnp
from jax import lax
from jax.experimental import pallas as pl
from jax.experimental.pallas import tpu as pltpu
from jax.sharding import Mesh
from jax.sharding import PartitionSpec as P

NX, NZ, NC = 4, 8, 2
HD = 128
GROUPS = 8
ROWS = 64
PCOLS = GROUPS * ROWS
COLS = 2 * PCOLS
BLOCKS = NX * NZ * NC
KEYS = BLOCKS * ROWS
HALF = KEYS // 2
CHUNK = NZ * ROWS
CG = 256
EXTRA = 8
TAIL = 16
INTERPRET = False
epsilon = 1e-06
masked_value = -1e30
SCALING = 1.0 / math.sqrt(HD)
EXP_SCALE = SCALING * math.log2(math.e)


def unit_rows(values):
    inverse = lax.rsqrt(jnp.mean(values * values, axis=-1, keepdims=True) + epsilon)
    return values * inverse, inverse


def norm_back(unit, inverse, grads, gain):
    scaled = grads * gain
    return inverse * (scaled - unit * jnp.mean(unit * scaled, axis=-1, keepdims=True))


def mm(left, right):
    return jnp.dot(left, right, preferred_element_type=jnp.float32)


def two_heads(ref, pair):
    first = ref[:, 2 * pair * HD : (2 * pair + 1) * HD]
    second = ref[:, (2 * pair + 1) * HD : (2 * pair + 2) * HD]
    return jnp.concatenate([first.astype(jnp.float32), second.astype(jnp.float32)], axis=0)


def prepare_kernel(
    pq_in, pg_in, po_in, rq_in, rg_in, ro_in, gain_in, qn, qn_t, gr, gr_t, delta, held, qgain, sems
):
    f32, bf16 = jnp.float32, jnp.bfloat16
    copies = [
        pltpu.make_async_copy(ref, held.at[i], sems.at[i])
        for i, ref in enumerate((pq_in, rq_in, pg_in, rg_in, po_in, ro_in))
    ]
    copies.append(pltpu.make_async_copy(gain_in, qgain, sems.at[len(copies)]))
    for copy in copies:
        copy.start()
    for copy in copies:
        copy.wait()
    gain_q = qgain[...]
    for part in range(2):
        q, g, o = held.at[part], held.at[2 + part], held.at[4 + part]
        for pair in range(GROUPS // 2):
            r0 = part * PCOLS + pair * 2 * ROWS
            rows = slice(r0, r0 + 2 * ROWS)
            unit, _ = unit_rows(two_heads(q, pair))
            normed = (unit * gain_q).astype(bf16)
            qn[rows, :] = normed
            qn_t[:, rows] = normed.astype(f32).T.astype(bf16)
            grads = two_heads(g, pair)
            gr[rows, :] = grads.astype(bf16)
            gr_t[:, rows] = grads.T.astype(bf16)
            product = grads * two_heads(o, pair)
            delta[:, rows] = jnp.sum(product.T, axis=0, keepdims=True)


def prepare(arrays, qgain):
    f32, bf16 = jnp.float32, jnp.bfloat16
    vmem = pl.BlockSpec(memory_space=pltpu.VMEM)
    out_shape = (
        jax.ShapeDtypeStruct((COLS, HD), bf16),
        jax.ShapeDtypeStruct((HD, COLS), bf16),
        jax.ShapeDtypeStruct((COLS, HD), bf16),
        jax.ShapeDtypeStruct((HD, COLS), bf16),
        jax.ShapeDtypeStruct((1, COLS), f32),
    )
    return pl.pallas_call(
        prepare_kernel,
        out_shape=out_shape,
        in_specs=[pl.BlockSpec(memory_space=pl.ANY)] * (len(arrays) + 1),
        out_specs=tuple([vmem] * len(out_shape)),
        scratch_shapes=[
            pltpu.VMEM((len(arrays), ROWS, GROUPS * HD), bf16),
            pltpu.VMEM((1, HD), f32),
            pltpu.SemaphoreType.DMA((len(arrays) + 1,)),
        ],
        compiler_params=pltpu.CompilerParams(vmem_limit_bytes=8 * 1024 * 1024),
        cost_estimate=pl.CostEstimate(flops=COLS * HD * 40, bytes_accessed=2 << 20, transcendentals=0),
        interpret=INTERPRET,
    )(*arrays, qgain)


def attention_kernel(
    info, own_in, other_in, kgain_in, rk_in, rv_in, qn_in, qn_t_in, gr_in, gr_t_in, delta_in, qgain_in,
    pq_in, rq_in, keep, send, terms, pdq, rdq, rdk, rdv,
    kn, kn_t, vals, kunit, rkn, rkn_t, probs, rprobs, maxima, top, total, factor, dq_t, held, rk, rv,
    weights_b, dscores_b, qn, qn_t, gr, gr_t, delta, qgain, kgain, kv_own, kv_other, sems,
):
    f32, bf16 = jnp.float32, jnp.bfloat16
    kv_refs = (kv_own, kv_other)
    moves = (
        (own_in, kv_own),
        (other_in, kv_other),
        (kgain_in, kgain),
        (rk_in, rk),
        (rv_in, rv),
        (qn_in, qn),
        (qn_t_in, qn_t),
        (gr_in, gr),
        (gr_t_in, gr_t),
        (delta_in, delta),
        (qgain_in, qgain),
        (pq_in, held.at[0]),
        (rq_in, held.at[1]),
    )
    copies = [pltpu.make_async_copy(src, dst, sems.at[i]) for i, (src, dst) in enumerate(moves)]
    for copy in copies:
        copy.start()
    for copy in copies[:3]:
        copy.wait()
    gain_k = kgain[...]

    k0 = 0
    for ref in kv_refs:
        for at in range(0, ref.shape[0], CHUNK):
            rows = slice(k0, k0 + CHUNK)
            unit, _ = unit_rows(ref[at : at + CHUNK, :HD].astype(f32))
            normed = (unit * gain_k).astype(bf16)
            kunit[rows, :] = unit
            kn[rows, :] = normed
            kn_t[k0 // CHUNK] = normed.astype(f32).T.astype(bf16)
            vals[rows, :] = ref[at : at + CHUNK, HD:]
            k0 += CHUNK

    for copy in copies[3:]:
        copy.wait()
    gain_q = qgain[...]
    runit, rinv = unit_rows(rk[...].astype(f32))
    rnormed = (runit * gain_k).astype(bf16)
    rkn[...] = rnormed
    rkn_t[...] = rnormed.astype(f32).T.astype(bf16)

    scores = mm(rkn[...], qn_t[:, PCOLS:]) * EXP_SCALE
    key_at = lax.broadcasted_iota(jnp.int32, (ROWS, PCOLS), 0)
    query_at = lax.broadcasted_iota(jnp.int32, (ROWS, PCOLS), 1) & (ROWS - 1)
    scores = jnp.where(key_at <= query_at, scores, masked_value)
    first = jnp.max(scores, axis=0, keepdims=True)
    raised = jnp.exp2(scores - first)
    rprobs[...] = raised
    rfirst = first
    top[:, :PCOLS] = jnp.full((1, PCOLS), masked_value, f32)
    total[:, :PCOLS] = jnp.zeros((1, PCOLS), f32)
    top[:, PCOLS:] = first
    total[:, PCOLS:] = jnp.sum(raised, axis=0, keepdims=True)

    my_x, my_z, my_core = info[1], info[2], info[3]

    def first_pass(j, _):
        at = pl.multiple_of(j * CHUNK, CHUNK)
        key_x = lax.rem(j, NX)
        key_core = jnp.where(j < NX, my_core, 1 - my_core)

        def tile(c0, masked):
            cols = slice(c0, c0 + CG)
            scores = mm(kn[pl.ds(at, CHUNK), :], qn_t[:, cols]) * EXP_SCALE
            if masked:
                row = lax.broadcasted_iota(jnp.int32, (CHUNK, 1), 0)
                key_block = (key_x * NZ + row // ROWS) * NC + key_core
                key_pos = key_block * ROWS + (row & (ROWS - 1))
                query_pos = lax.broadcasted_iota(jnp.int32, (1, CG), 1) & (ROWS - 1)
                query_pos = query_pos + ((my_x * NZ + my_z) * NC + my_core) * ROWS
                scores = jnp.where(key_pos <= query_pos, scores, masked_value)
            old = top[:, cols]
            new = jnp.maximum(old, jnp.max(scores, axis=0, keepdims=True))
            raised = jnp.exp2(scores - new)
            probs[pl.ds(at, CHUNK), cols] = raised
            total[:, cols] = total[:, cols] * jnp.exp2(old - new) + jnp.sum(
                raised, axis=0, keepdims=True
            )
            top[:, cols] = new
            maxima[j, :, cols] = new

        @pl.when(key_x < my_x)
        def _():
            for c0 in range(0, COLS, CG):
                tile(c0, False)

        @pl.when(key_x >= my_x)
        def _():
            for c0 in range(0, COLS, CG):
                tile(c0, c0 < PCOLS)

        return 0

    lax.fori_loop(0, KEYS // CHUNK, first_pass, 0)

    column = lax.broadcasted_iota(jnp.int32, (1, COLS), 1)
    living = (column < PCOLS) | ((column & (ROWS - 1)) < info[0])
    factor[...] = jnp.where(living, 1.0 / total[...], 0.0)
    dq_t[...] = jnp.zeros_like(dq_t)

    def second_pass(out, base, j, carry):
        key_terms, largest_k, largest_v = carry
        at = pl.multiple_of(j * CHUNK, CHUNK)
        here = pl.multiple_of((j - base) * CHUNK, CHUNK)
        values = vals[pl.ds(at, CHUNK), :]
        keys_t = kn_t[j]
        for c0 in range(0, COLS, CG):
            cols = slice(c0, c0 + CG)
            scale = jnp.exp2(maxima[j, :, cols] - top[:, cols]) * factor[:, cols]
            weights = probs[pl.ds(at, CHUNK), cols] * scale
            dweights = mm(values, gr_t[:, cols])
            weights_b[:, cols] = weights.astype(bf16)
            dscores_b[:, cols] = (weights * (dweights - delta[:, cols])).astype(bf16)
        dvalue = mm(weights_b[...], gr[...])
        dkey = mm(dscores_b[...], qn[...])
        dq_t[...] = dq_t[...] + mm(keys_t, dscores_b[...])
        dkey = dkey * SCALING
        out[pl.ds(here, CHUNK), :HD] = dkey
        out[pl.ds(here, CHUNK), HD:] = dvalue
        products = dkey * kunit[pl.ds(at, CHUNK), :]
        eights = (CHUNK // 8, 8, HD)
        return (
            key_terms + jnp.sum(products.reshape(eights), axis=0),
            jnp.maximum(largest_k, jnp.max(jnp.abs(dkey).reshape(eights), axis=0)),
            jnp.maximum(largest_v, jnp.max(jnp.abs(dvalue).reshape(eights), axis=0)),
        )

    half = HALF // CHUNK
    zero = jnp.zeros((8, HD), f32)
    key_terms = zero
    for out, base in ((send, half), (keep, 0)):
        key_terms, largest_k, largest_v = lax.fori_loop(
            base, base + half, functools.partial(second_pass, out, base), (key_terms, zero, zero)
        )
        out[HALF:, :HD] = jnp.broadcast_to(jnp.max(largest_k, axis=0, keepdims=True), (EXTRA, HD))
        out[HALF:, HD:] = jnp.broadcast_to(jnp.max(largest_v, axis=0, keepdims=True), (EXTRA, HD))

    right = slice(PCOLS, COLS)
    scale = jnp.exp2(rfirst - top[:, right]) * factor[:, right]
    weights = rprobs[...] * scale
    dweights = mm(rv[...], gr_t[:, right])
    dscores = (weights * (dweights - delta[:, right])).astype(bf16)
    rdv[...] = mm(weights.astype(bf16), gr[right, :]).astype(bf16)
    dkey = mm(dscores, qn[right, :]) * SCALING
    rdk[...] = norm_back(runit, rinv, dkey, gain_k).astype(bf16)
    dq_t[:, right] = dq_t[:, right] + mm(rkn_t[...], dscores)
    key_terms = jnp.sum(key_terms, axis=0, keepdims=True)
    key_terms = key_terms + jnp.sum(dkey * runit, axis=0, keepdims=True)

    query_terms = jnp.zeros((1, HD), f32)
    for part, out in enumerate((pdq, rdq)):
        q = held.at[part]
        for pair in range(GROUPS // 2):
            r0 = part * PCOLS + pair * 2 * ROWS
            unit, inverse = unit_rows(two_heads(q, pair))
            dquery = dq_t[:, r0 : r0 + 2 * ROWS].T * SCALING
            query_terms = query_terms + jnp.sum(dquery * unit, axis=0, keepdims=True)
            raw = norm_back(unit, inverse, dquery, gain_q).astype(bf16)
            out[:, 2 * pair * HD : (2 * pair + 1) * HD] = raw[:ROWS]
            out[:, (2 * pair + 1) * HD : (2 * pair + 2) * HD] = raw[ROWS:]

    terms[:, :HD] = jnp.broadcast_to(query_terms, (EXTRA, HD))
    terms[:, HD:] = jnp.broadcast_to(key_terms, (EXTRA, HD))


def attention(info, arrays):
    f32, bf16 = jnp.float32, jnp.bfloat16
    vmem = pl.BlockSpec(memory_space=pltpu.VMEM)
    smem = pl.BlockSpec(memory_space=pltpu.SMEM)
    out_shape = (
        jax.ShapeDtypeStruct((HALF + EXTRA, 2 * HD), f32),
        jax.ShapeDtypeStruct((HALF + EXTRA, 2 * HD), f32),
        jax.ShapeDtypeStruct((EXTRA, 2 * HD), f32),
        jax.ShapeDtypeStruct((ROWS, GROUPS * HD), bf16),
        jax.ShapeDtypeStruct((ROWS, GROUPS * HD), bf16),
        jax.ShapeDtypeStruct((ROWS, HD), bf16),
        jax.ShapeDtypeStruct((ROWS, HD), bf16),
    )
    chunks = KEYS // CHUNK
    scratch = [
        pltpu.VMEM((KEYS, HD), bf16),
        pltpu.VMEM((chunks, HD, CHUNK), bf16),
        pltpu.VMEM((KEYS, HD), bf16),
        pltpu.VMEM((KEYS, HD), f32),
        pltpu.VMEM((ROWS, HD), bf16),
        pltpu.VMEM((HD, ROWS), bf16),
        pltpu.VMEM((KEYS, COLS), f32),
        pltpu.VMEM((ROWS, PCOLS), f32),
        pltpu.VMEM((chunks, 1, COLS), f32),
        pltpu.VMEM((1, COLS), f32),
        pltpu.VMEM((1, COLS), f32),
        pltpu.VMEM((1, COLS), f32),
        pltpu.VMEM((HD, COLS), f32),
        pltpu.VMEM((2, ROWS, GROUPS * HD), bf16),
        pltpu.VMEM((ROWS, HD), bf16),
        pltpu.VMEM((ROWS, HD), bf16),
        pltpu.VMEM((CHUNK, COLS), bf16),
        pltpu.VMEM((CHUNK, COLS), bf16),
        pltpu.VMEM((COLS, HD), bf16),
        pltpu.VMEM((HD, COLS), bf16),
        pltpu.VMEM((COLS, HD), bf16),
        pltpu.VMEM((HD, COLS), bf16),
        pltpu.VMEM((1, COLS), f32),
        pltpu.VMEM((1, HD), f32),
        pltpu.VMEM((1, HD), f32),
        pltpu.VMEM((HALF, 2 * HD), bf16),
        pltpu.VMEM((HALF, 2 * HD), bf16),
        pltpu.SemaphoreType.DMA((len(arrays),)),
    ]
    return pl.pallas_call(
        attention_kernel,
        out_shape=out_shape,
        in_specs=[smem] + [pl.BlockSpec(memory_space=pl.ANY)] * len(arrays),
        out_specs=tuple([vmem] * len(out_shape)),
        scratch_shapes=scratch,
        compiler_params=pltpu.CompilerParams(vmem_limit_bytes=42 * 1024 * 1024),
        cost_estimate=pl.CostEstimate(
            flops=10 * KEYS * COLS * HD, bytes_accessed=8 << 20, transcendentals=KEYS * COLS
        ),
        interpret=INTERPRET,
    )(info, *arrays)


def exchange(array, axis):
    return lax.all_to_all(array, axis, 0, 0, tiled=True)


def exchange_copies(array, axis):
    count = lax.axis_size(axis)
    copies = jnp.broadcast_to(array[None], (count,) + array.shape)
    return exchange(copies.reshape((-1,) + array.shape[1:]), axis)


def exchange_halves(halves, axis):
    got = exchange(halves.reshape(-1, 2 * HD), axis)
    return got.astype(jnp.float32).reshape(halves.shape)


def swap_core(array):
    return lax.ppermute(array, "core", [(0, 1), (1, 0)])


def pack_message(message, rows, count, blocks, largest, terms):
    exponent = jnp.clip(jnp.floor(jnp.log2(jnp.maximum(largest, 1e-37))), -100.0, 100.0)
    scale = jnp.exp2(14.0 - exponent)
    term_exponent = jnp.clip(
        jnp.floor(jnp.log2(jnp.maximum(jnp.abs(terms), 1e-37))), -100.0, 100.0
    )
    scaled = terms * jnp.exp2(14.0 - term_exponent)
    high = scaled.astype(jnp.bfloat16).astype(jnp.float32)
    low = (scaled - high) * 256.0
    row = lax.broadcasted_iota(jnp.int32, (TAIL, 2 * HD), 0)
    tail = jnp.where(row == 2, exponent, term_exponent)
    tail = jnp.where(row == 0, high, jnp.where(row == 1, low, tail))
    for i in range(count):
        message[i, :rows] = blocks(i) * scale
        message[i, rows:] = tail


def unpack_message(message, rows, count):
    total = jnp.zeros((rows, 2 * HD), jnp.float32)
    terms = jnp.zeros((1, 2 * HD), jnp.float32)
    for i in range(count):
        tail = message[i, rows:]
        total = total + message[i, :rows] * jnp.exp2(tail[2:3] - 14.0)
        terms = terms + (tail[0:1] + tail[1:2] * (1.0 / 256.0)) * jnp.exp2(tail[3:4] - 14.0)
    return total, terms


def first_stage_kernel(keep, got, terms, message):
    rows = NZ * ROWS
    largest = keep[HALF : HALF + 1, :] + got[HALF : HALF + 1, :]

    def blocks(i):
        return keep[i * rows : (i + 1) * rows, :] + got[i * rows : (i + 1) * rows, :]

    pack_message(message, rows, NX, blocks, largest, terms[0:1, :])


def second_stage_kernel(got, message):
    total, terms = unpack_message(got, NZ * ROWS, NX)
    largest = jnp.max(jnp.abs(total), axis=0, keepdims=True)
    pack_message(message, ROWS, NZ, lambda i: total[i * ROWS : (i + 1) * ROWS], largest, terms)


def last_stage_kernel(got, keys, kgain, pdk, pdv, query_terms, key_terms):
    total, terms = unpack_message(got, ROWS, NZ)
    unit, inverse = unit_rows(keys[...].astype(jnp.float32))
    pdk[...] = norm_back(unit, inverse, total[:, :HD], kgain[...]).astype(jnp.bfloat16)
    pdv[...] = total[:, HD:].astype(jnp.bfloat16)
    query_terms[...] = terms[:, :HD]
    key_terms[...] = terms[:, HD:]


def small_kernel(body, out_shape, *arrays):
    vmem = pl.BlockSpec(memory_space=pltpu.VMEM)
    outs = vmem if isinstance(out_shape, jax.ShapeDtypeStruct) else tuple([vmem] * len(out_shape))
    return pl.pallas_call(
        body,
        out_shape=out_shape,
        in_specs=[vmem] * len(arrays),
        out_specs=outs,
        compiler_params=pltpu.CompilerParams(vmem_limit_bytes=16 * 1024 * 1024),
        cost_estimate=pl.CostEstimate(flops=1 << 20, bytes_accessed=4 << 20, transcendentals=0),
        interpret=INTERPRET,
    )(*arrays)


def per_device(
    prompt_query,
    prompt_key,
    prompt_value,
    prompt_out,
    prompt_grad,
    response_query,
    response_key,
    response_value,
    response_out,
    response_grad,
    lengths,
    query_gain,
    key_gain,
):
    place = [lax.axis_index(name).astype(jnp.int32)[None] for name in ("x", "z", "core")]
    info = jnp.concatenate([lengths, *place])
    qgain, kgain = query_gain.reshape(1, HD), key_gain.reshape(1, HD)

    local = jnp.concatenate([prompt_key, prompt_value], axis=1)
    own = exchange_copies(local, ("x", "z"))
    raw = [prompt_query, prompt_grad, prompt_out, response_query[0], response_grad[0], response_out[0]]
    prepared = prepare(raw, qgain)
    own, prepared = lax.optimization_barrier((own, prepared))
    other = swap_core(own)
    keep, give, terms, pdq, rdq, rdk, rdv = attention(
        info,
        [
            own,
            other,
            kgain,
            response_key[0],
            response_value[0],
            *prepared,
            qgain,
            prompt_query,
            response_query[0],
        ],
    )

    got = swap_core(give)
    terms = exchange_copies(terms, ("core", "head")).reshape(-1, EXTRA, 2 * HD).sum(axis=0)
    rows = NZ * ROWS + TAIL
    message = small_kernel(
        first_stage_kernel, jax.ShapeDtypeStruct((NX, rows, 2 * HD), jnp.float32), keep, got, terms
    )
    message = exchange_halves(message.astype(jnp.float16), "x")
    rows = ROWS + TAIL
    message = small_kernel(
        second_stage_kernel, jax.ShapeDtypeStruct((NZ, rows, 2 * HD), jnp.float32), message
    )
    message = exchange_halves(message.astype(jnp.float16), "z")
    block = jax.ShapeDtypeStruct((ROWS, HD), jnp.bfloat16)
    gain = jax.ShapeDtypeStruct((1, HD), jnp.float32)
    pdk, pdv, query_total, key_total = small_kernel(
        last_stage_kernel, (block, block, gain, gain), message, prompt_key, kgain
    )
    return pdq, pdk, pdv, rdq[None], rdk[None], rdv[None], query_total[0], key_total[0]


def solution(mesh):
    heads = mesh.devices.shape[1]
    mesh = Mesh(mesh.devices.reshape(NX, NZ, NC, heads), ("x", "z", "core", "head"))
    dp = ("x", "z", "core")
    columns, stacked = P(dp, "head"), P(dp, None, "head")
    in_specs = (columns,) * 5 + (stacked,) * 5 + (P(dp), P(), P())
    out_specs = (columns,) * 3 + (stacked,) * 3 + (P(), P())
    return jax.shard_map(
        per_device, mesh=mesh, in_specs=in_specs, out_specs=out_specs, check_vma=False
    )
```
